256 devices in a mesh: ep: 64 (over z_lo, x, y), tp: 4 (over z_hi, core).
Axes of the slice: x: 4, y: 4, z: 8 (z_hi: 2, z_lo: 4; z = z_hi * 4 + z_lo), core: 2. Of those that a mesh axis runs over, the one named last changes fastest.
Arguments:
- activations: float32 [256, 256, 1280], P(('ep', 'tp')), may hold values from -6 to 6
- out_grad: float32 [256, 256, 1280], P(('ep', 'tp')), may hold values from -6 to 6
- slot_out: float32 [256, 128, 1280], P(('ep', 'tp')), may hold values from -6 to 6
- slot_proj: float32 [1280, 128], replicated, may hold values from -1.5625 to 1.5625
- w_in: bfloat16 [64, 1280, 5120], P('ep', None, 'tp'), may hold values from -0.15625 to 0.15625
- w_out: bfloat16 [64, 5120, 1280], P('ep', 'tp'), may hold values from -0.078125 to 0.078125
Outputs:
- d_acts: float32 [256, 256, 1280], P(('ep', 'tp'))
- d_proj: float32 [1280, 128], P('tp', 'ep')
The draws below stay inside these ranges and needn't reach their ends.
All inputs are finite; a program needn't handle non-finite values.
Results may differ from the reference program's by a relative error of at most 0.0025.
Values may be sent and summed in bfloat16 or wider, within the bound.
A program may use at most 128 MiB of HBM per device.

```python
import math
import jax
import jax.numpy as jnp
from jax import lax

D = 1280
FF = 5120
PATCHES = 256
SLOTS = 2
EXPERTS = 64
N_SLOTS = 128
IMAGES = 256


def shared_acts(key):
    return jnp.clip(jax.random.normal(key, (IMAGES, PATCHES, D), jnp.float32), -6.0, 6.0)


def draw_activations(key, part):
    return shared_acts(key)


def draw_slot_proj(key, part):
    key = jax.random.fold_in(key, 11)
    values = jax.random.normal(key, (D, N_SLOTS), jnp.float32)
    values = jnp.clip(values, -6.0, 6.0) * (3.0 / math.sqrt(D))
    return values


def shard_levels(own_key, shape, pieces, least, high):
    def one(position, parts):
        steps = jax.random.uniform(jax.random.fold_in(jax.random.fold_in(own_key, 6), position), (parts,), jnp.float32, least / len(pieces), high / len(pieces))
        return jnp.repeat(jnp.exp(steps), shape[position] // parts).reshape((-1,) + (1,) * (len(shape) - position - 1))

    factor_of = one(*pieces[0])
    for cut in pieces[1:]:
        factor_of = factor_of * one(*cut)
    return factor_of


def noise(key, dims, width, reach, pieces=(), dtype=jnp.bfloat16):
    entries = width * jax.random.normal(key, dims, jnp.float32)
    if pieces:
        entries = entries * shard_levels(key, dims, pieces, -0.22, 0.18)
    return jnp.clip(entries, -reach, reach).astype(dtype)


def setup_inputs(seed: int = 0) -> dict:
    splits = jax.random.split(jax.random.key(seed), 7)
    return {
        "activations": draw_activations(jax.random.fold_in(splits[6], 71), 0),
        "out_grad": noise(splits[1], (IMAGES, PATCHES, D), 1.0, 6.0, ((0, 256),), jnp.float32),
        "slot_out": noise(splits[2], (IMAGES, N_SLOTS, D), 1.0, 6.0, ((0, 256),), jnp.float32),
        "slot_proj": draw_slot_proj(jax.random.fold_in(splits[6], 71), 0),
        "w_in": noise(splits[4], (EXPERTS, D, FF), D ** -0.5, 0.15625, ((0, 64), (2, 4))),
        "w_out": noise(splits[5], (EXPERTS, FF, D), FF ** -0.5, 0.078125, ((0, 64), (1, 4))),
    }


def gelu_slope(pre_act):
    normal_cdf = 0.5 * (1.0 + lax.erf(pre_act * 0.7071067811865476))
    density = jnp.exp(-0.5 * pre_act * pre_act) * 0.3989422804014327
    return normal_cdf + pre_act * density

def expert_grad(operands):
    rows_in, rows_grad, first_proj, second_proj = operands
    pre_act = jnp.dot(rows_in, first_proj, preferred_element_type=jnp.float32)
    hidden_grad = jnp.dot(rows_grad, second_proj.T, preferred_element_type=jnp.float32)
    pre_grad = (hidden_grad * gelu_slope(pre_act)).astype(jnp.bfloat16)
    return jnp.dot(pre_grad, first_proj.T, preferred_element_type=jnp.float32)

def regroup(values):
    return values.reshape(IMAGES, EXPERTS, SLOTS, D).transpose(1, 0, 2, 3).reshape(EXPERTS, IMAGES * SLOTS, D)

def reference(activations, out_grad, slot_out, slot_proj, w_in, w_out):
    highest = lax.Precision.HIGHEST
    logits = jnp.einsum('bmd,dn->bmn', activations, slot_proj, precision=highest)
    dispatch = jax.nn.softmax(logits, axis=1)
    combine = jax.nn.softmax(logits, axis=2)
    slot_in = jnp.einsum('bmn,bmd->bnd', dispatch, activations, precision=highest).astype(jnp.bfloat16)
    slot_grad = jnp.einsum('bmn,bmd->bnd', combine, out_grad, precision=highest).astype(jnp.bfloat16)
    per_expert = lax.map(expert_grad, (regroup(slot_in), regroup(slot_grad), w_in, w_out))
    slot_in_grad = per_expert.reshape(EXPERTS, IMAGES, SLOTS, D).transpose(1, 0, 2, 3).reshape(IMAGES, N_SLOTS, D)
    comb_grad = jnp.einsum('bmd,bnd->bmn', out_grad, slot_out, precision=highest)
    disp_grad = jnp.einsum('bmd,bnd->bmn', activations, slot_in_grad, precision=highest)
    logit_grad = combine * (comb_grad - lax.optimization_barrier(jnp.sum(comb_grad * combine, axis=2, keepdims=True)))
    logit_grad = logit_grad + dispatch * (disp_grad - lax.optimization_barrier(jnp.sum(disp_grad * dispatch, axis=1, keepdims=True)))
    d_acts = jnp.einsum('bmn,bnd->bmd', dispatch, slot_in_grad, precision=highest)
    d_acts = d_acts + jnp.einsum('bmn,dn->bmd', logit_grad, slot_proj, precision=highest)
    d_proj = jnp.einsum('bmd,bmn->dn', activations, logit_grad, precision=highest)
    return (d_acts, d_proj)
```

```python
import jax
import jax.numpy as jnp
from jax import lax
from jax.sharding import PartitionSpec as P


def gelu_slope(pre_act):
    normal_cdf = 0.5 * (1.0 + lax.erf(pre_act * 0.7071067811865476))
    density = jnp.exp(-0.5 * pre_act * pre_act) * 0.3989422804014327
    return normal_cdf + pre_act * density


def send_back(summed):
    return lax.all_to_all(summed, "ep", split_axis=1, concat_axis=1, tiled=True)


def contract_last(left, right):
    return lax.dot_general(
        left, right, (((1,), (1,)), ((), ())), preferred_element_type=jnp.float32
    )


def local(activations, out_grad, slot_out, slot_proj, w_in, w_out):
    highest = lax.Precision.HIGHEST
    images = activations.shape[0]
    model_width = activations.shape[2]
    slot_count = slot_proj.shape[1]
    ep_count = lax.axis_size("ep")
    tp_count = lax.axis_size("tp")
    logits = jnp.einsum("bmd,dn->bmn", activations, slot_proj, precision=highest)
    dispatch = jax.nn.softmax(logits, axis=1)
    combine = jax.nn.softmax(logits, axis=2)
    slot_in = jnp.einsum("bmn,bmd->bnd", dispatch, activations, precision=highest).astype(
        jnp.bfloat16
    )
    slot_grad = jnp.einsum("bmn,bmd->bnd", combine, out_grad, precision=highest).astype(
        jnp.bfloat16
    )
    grouped = (images, ep_count, slot_count // ep_count, model_width)
    first_proj = w_in[0]
    second_proj = w_out[0]
    recv_in = lax.all_to_all(
        slot_in.reshape(grouped), "ep", split_axis=1, concat_axis=1, tiled=True
    )
    recv_grad = lax.all_to_all(
        slot_grad.reshape(grouped), "ep", split_axis=1, concat_axis=1, tiled=True
    )
    layout = recv_in.shape
    all_in = lax.all_gather(recv_in, "tp", axis=0, tiled=True)
    all_grad = lax.all_gather(recv_grad, "tp", axis=0, tiled=True)
    pre_act = jnp.dot(
        all_in.reshape(-1, model_width), first_proj, preferred_element_type=jnp.float32
    )
    hidden_grad = contract_last(all_grad.reshape(-1, model_width), second_proj)
    pre_grad = (hidden_grad * gelu_slope(pre_act)).astype(jnp.bfloat16)
    summed = lax.psum_scatter(
        contract_last(pre_grad, first_proj), "tp", scatter_dimension=0, tiled=True
    )
    returned = send_back(summed.reshape(layout))
    slot_in_grad = returned.reshape(images, slot_count, model_width)
    comb_grad = jnp.einsum("bmd,bnd->bmn", out_grad, slot_out, precision=highest)
    disp_grad = jnp.einsum("bmd,bnd->bmn", activations, slot_in_grad, precision=highest)
    logit_grad = combine * (comb_grad - jnp.sum(comb_grad * combine, axis=2, keepdims=True))
    logit_grad = logit_grad + dispatch * (
        disp_grad - jnp.sum(disp_grad * dispatch, axis=1, keepdims=True)
    )
    d_acts = jnp.einsum("bmn,bnd->bmd", dispatch, slot_in_grad, precision=highest)
    d_acts = d_acts + jnp.einsum("bmn,dn->bmd", logit_grad, slot_proj, precision=highest)
    proj_term = jnp.einsum("bmn,bmd->nd", logit_grad, activations, precision=highest)
    row_count = model_width // tp_count
    col_count = slot_count // ep_count
    parts = lax.all_to_all(
        proj_term.reshape(ep_count, col_count, model_width),
        "ep",
        split_axis=0,
        concat_axis=0,
        tiled=True,
    )
    summed_proj = lax.psum(jnp.sum(parts, axis=0), "tp")
    d_proj = lax.dynamic_slice(
        summed_proj, (0, lax.axis_index("tp") * row_count), (col_count, row_count)
    ).T
    return (d_acts, d_proj)


def solution(mesh):
    placed = (
        P(("ep", "tp"), None, None),
        P(("ep", "tp"), None, None),
        P(("ep", "tp"), None, None),
        P(),
        P("ep", None, "tp"),
        P("ep", "tp", None),
    )
    return jax.shard_map(
        local,
        mesh=mesh,
        in_specs=placed,
        out_specs=(P(("ep", "tp"), None, None), P("tp", "ep")),
        check_vma=False,
    )
```

```python
import functools

import jax
import jax.numpy as jnp
from jax import lax
from jax.experimental import pallas as pl
from jax.experimental.pallas import tpu as pltpu
from jax.sharding import PartitionSpec as P

MESH = pl.DeviceIdType.MESH
F32 = jnp.float32
BF16 = jnp.bfloat16
D = 1280
HALF = 640
TOKENS = 256
SLOTS = 128
ROWS = 256
PLANE = 16
RING = 8
FORWARD = (
    (0, 0, 128), (0, 128, 256), (0, 384, 256),
    (1, 0, 256), (1, 256, 256), (1, 512, 128),
)
BACK = ((0, 256), (256, 256), (512, 256), (768, 256), (1024, 256))
NF, NB = len(FORWARD), len(BACK)


def gelu_slope(pre_act):
    normal_cdf = 0.5 * (1.0 + lax.erf(pre_act * 0.7071067811865476))
    density = jnp.exp(-0.5 * pre_act * pre_act) * 0.3989422804014327
    return normal_cdf + pre_act * density


def dot_nn(a, b):
    return jnp.dot(a, b, preferred_element_type=F32)


def dot_nt(a, b):
    return lax.dot_general(a, b, (((1,), (1,)), ((), ())), preferred_element_type=F32)


def split(a):
    high = a.astype(BF16)
    return high, (a - high.astype(F32)).astype(BF16)


def three(dot, a, b):
    return dot(a[0], b[0]) + (dot(a[0], b[1]) + dot(a[1], b[0]))


def iota2(shape, axis):
    return lax.broadcasted_iota(jnp.int32, shape, axis)


def one_hot(condition):
    return jnp.where(condition, 1.0, 0.0).astype(BF16)


def kernel(
    acts_hbm, og_hbm, so_hbm, sp_hbm, wi_hbm, wo_hbm,
    dacts_hbm, dproj_ref,
    acts, og, so, sp, wi, wo,
    acts_s, og_s, so_s, sp_s, disp_s, comb, disp, comb_term, disp_grad, dacts,
    send, plane_in, ring_out, ring_in, other_in,
    acc, pre_grad, part, part_in, back_out, back_in, back_send, sig,
    dp, dp_in, dp_sum, dp_plane, dp_ring, dp_back,
    load_sem, fps, fpr, fzs, fzr, fcs, fcr, bcs, bcr, bzs, bzr, bps, bpr, dps, dpr, out_sem,
):
    ep, tp = lax.axis_index("ep"), lax.axis_index("tp")
    z_lo, pos = lax.div(ep, 16), lax.rem(ep, 16)
    x, y = lax.div(pos, 4), lax.rem(pos, 4)
    z_hi, core = lax.div(tp, 2), lax.rem(tp, 2)
    z = z_hi * 4 + z_lo
    other = {"ep": ep, "tp": z_hi * 2 + (1 - core)}

    def plane_peer(q):
        there = lax.rem(x + lax.div(q, 4), 4) * 4 + lax.rem(y + lax.rem(q, 4), 4)
        return there, {"ep": z_lo * 16 + there, "tp": tp}

    def ring_peer(q):
        there = lax.rem(z + q, RING)
        lo = lax.rem(there, 4)
        return there, lo, {"ep": lo * 16 + pos, "tp": lax.div(there, 4) * 2 + core}

    def remote(src, dst, send_sem, recv_sem, device):
        return pltpu.make_async_remote_copy(
            src_ref=src, dst_ref=dst, send_sem=send_sem, recv_sem=recv_sem,
            device_id=device, device_id_type=MESH,
        )

    def wait_bytes(ref, sem):
        pltpu.make_async_copy(ref, ref, sem).wait()

    loads = []
    pairs = ((sp_hbm, sp), (acts_hbm, acts), (og_hbm, og), (so_hbm, so), (wi_hbm, wi), (wo_hbm, wo))
    for k, (src, dst) in enumerate(pairs):
        loads.append(pltpu.make_async_copy(src, dst, load_sem.at[k]))
        loads[-1].start()
    load_sp, load_acts, load_og, load_so, load_wi, load_wo = loads

    barrier = pltpu.get_barrier_semaphore()

    def greet_plane(q, carry):
        pl.semaphore_signal(barrier, inc=1, device_id=plane_peer(q)[1], device_id_type=MESH)
        return carry

    def greet_ring(q, carry):
        pl.semaphore_signal(barrier, inc=1, device_id=ring_peer(q)[2], device_id_type=MESH)
        return carry

    lax.fori_loop(1, PLANE, greet_plane, 0)
    lax.fori_loop(1, RING, greet_ring, 0)
    pl.semaphore_signal(barrier, inc=1, device_id=other, device_id_type=MESH)

    n, r = iota2((SLOTS, SLOTS), 0), iota2((SLOTS, SLOTS), 1)
    natural = lax.rem(lax.div(r, 2), 4) * 32 + lax.div(r, 8) * 2 + lax.rem(r, 2)
    to_order = one_hot(n == natural)
    natural_t = lax.rem(lax.div(n, 2), 4) * 32 + lax.div(n, 8) * 2 + lax.rem(n, 2)
    to_order_t = one_hot(r == natural_t)
    o, i = iota2((ROWS, ROWS), 0), iota2((ROWS, ROWS), 1)
    source = (
        lax.rem(lax.div(o, 2), 16) * 16 + lax.rem(lax.div(o, 32), 2) * 8
        + lax.div(o, 64) * 2 + lax.rem(o, 2)
    )
    regroup = one_hot(i == source)
    o, i = iota2((SLOTS, ROWS), 0), iota2((SLOTS, ROWS), 1)
    source = lax.rem(lax.div(o, 2), 4) * 32 + lax.div(o, 8) * 2 + lax.rem(o, 2)
    collect = one_hot(lax.rem(i, 128) == source)

    load_sp.wait()
    for k, part_of in enumerate(split(sp[...])):
        sp_s[k] = dot_nn(part_of, to_order).astype(BF16)
    load_acts.wait()
    acts_s[0], acts_s[1] = split(acts[...])
    logits = three(dot_nn, (acts_s[0], acts_s[1]), (sp_s[0], sp_s[1]))
    e = jnp.exp(logits - jnp.max(logits, axis=0, keepdims=True))
    dispatch = e / jnp.sum(e, axis=0, keepdims=True)
    disp[...] = dispatch
    disp_s[0], disp_s[1] = split(dispatch)
    e = jnp.exp(logits - jnp.max(logits, axis=1, keepdims=True))
    combine = e / jnp.sum(e, axis=1, keepdims=True)
    comb[...] = combine

    def slot_rows(kind, weights_t, values, col, width):
        halves = []
        for h in range(2):
            c = h * HALF + col
            rows = three(
                dot_nn, weights_t, (values[0, :, c : c + width], values[1, :, c : c + width])
            )
            halves.append(rows.reshape(PLANE, 8, width))
        both = jnp.concatenate(halves, axis=1).reshape(ROWS, width)
        send[kind, :, col : col + width] = both.astype(BF16)

    def plane_send(k):
        kind, col, width = FORWARD[k]

        def one(q, carry):
            there, device = plane_peer(q)
            remote(
                send.at[kind, pl.ds(there * 16, 16), pl.ds(col, width)],
                plane_in.at[kind, pl.ds(pos * 16, 16), pl.ds(col, width)],
                fps.at[k], fpr.at[k], device,
            ).start()
            return carry

        lax.fori_loop(1, PLANE, one, 0)
        plane_in[kind, pl.ds(pos * 16, 16), pl.ds(col, width)] = send[
            kind, pl.ds(pos * 16, 16), pl.ds(col, width)
        ]

    dispatch_t = split(dispatch.T)
    for k in range(NF):
        kind, col, width = FORWARD[k]
        if kind == 0:
            slot_rows(0, dispatch_t, acts_s, col, width)
            if k == 0:
                pl.semaphore_wait(barrier, PLANE - 1 + RING - 1 + 1)
            plane_send(k)

    load_og.wait()
    og_s[0], og_s[1] = split(og[...])
    combine_t = split(combine.T)
    for k in range(NF):
        kind, col, width = FORWARD[k]
        if kind == 1:
            slot_rows(1, combine_t, og_s, col, width)
            plane_send(k)

    for k in range(NF):
        kind, col, width = FORWARD[k]
        wait_bytes(plane_in.at[kind, pl.ds(0, 240), pl.ds(col, width)], fpr.at[k])
        moved = dot_nn(regroup, plane_in[kind, :, col : col + width])
        ring_out[kind, :, :, col : col + width] = moved.astype(BF16).reshape(8, 32, width)

        def one(q, carry):
            there, lo, device = ring_peer(q)
            remote(
                ring_out.at[kind, pl.ds(lo * 2, 2), :, pl.ds(col, width)],
                ring_in.at[kind, :, pl.ds(z * 32, 32), pl.ds(col, width)],
                fzs.at[k], fzr.at[k], device,
            ).start()
            return carry

        lax.fori_loop(1, RING, one, 0)
        ring_in[kind, :, pl.ds(z * 32, 32), pl.ds(col, width)] = ring_out[
            kind, pl.ds(z_lo * 2, 2), :, pl.ds(col, width)
        ]

    load_so.wait()
    for k, part_of in enumerate(split(so[...])):
        so_s[k] = dot_nn(to_order_t, part_of).astype(BF16)
    comb_grad = three(dot_nt, (og_s[0], og_s[1]), (so_s[0], so_s[1]))
    combine = comb[...]
    comb_term[...] = combine * (
        comb_grad - jnp.sum(comb_grad * combine, axis=1, keepdims=True)
    )

    load_wi.wait()
    load_wo.wait()

    def expert(k, rows_ref, own):
        kind, col, width = FORWARD[k]
        last = k == NF - 1

        def tile(t, carry):
            c = pl.multiple_of(t * 256, 256)
            total = None
            for h in range(2):
                rows = rows_ref[kind, h, :, col : col + width]
                d = h * HALF + col
                if kind == 0:
                    term = dot_nn(rows, wi[pl.ds(d, width), pl.ds(c, 256)])
                else:
                    term = dot_nt(rows, wo[pl.ds(c, 256), pl.ds(d, width)])
                total = term if total is None else total + term
            if col > 0:
                total = total + acc[kind, own, :, pl.ds(c, 256)]
            if kind == 0 and col + width == HALF:
                total = gelu_slope(total)
            if last:
                slope = acc[0, own, :, pl.ds(c, 256)]
                pre_grad[own, :, pl.ds(c, 256)] = (total * slope).astype(BF16)
            else:
                acc[kind, own, :, pl.ds(c, 256)] = total
            return carry

        lax.fori_loop(0, 5, tile, 0)

    for k in range(NF):
        kind, col, width = FORWARD[k]
        wait_bytes(ring_in.at[kind, :, pl.ds(0, 224), pl.ds(col, width)], fzr.at[k])
        across = remote(
            ring_in.at[kind, :, :, pl.ds(col, width)],
            other_in.at[kind, :, :, pl.ds(col, width)],
            fcs.at[k], fcr.at[k], other,
        )
        across.start()
        expert(k, ring_in, 0)
        across.wait_recv()
        expert(k, other_in, 1)

    def back_across(b):
        col, width = BACK[b]
        return remote(
            part.at[1, :, pl.ds(col, width)], part_in.at[:, pl.ds(col, width)],
            bcs.at[b], bcr.at[b], other,
        )

    def back_ring(b):
        col, width = BACK[b]
        back_across(b).wait_recv()
        both = part[0, :, col : col + width] + part_in[:, col : col + width]
        back_out[:, col : col + width] = both.astype(BF16)

        def one(q, carry):
            there, _, device = ring_peer(q)
            remote(
                back_out.at[pl.ds(there * 32, 32), pl.ds(col, width)],
                back_in.at[pl.ds(z * 32, 32), pl.ds(col, width)],
                bzs.at[b], bzr.at[b], device,
            ).start()
            return carry

        lax.fori_loop(1, RING, one, 0)
        back_in[pl.ds(z * 32, 32), pl.ds(col, width)] = back_out[
            pl.ds(z * 32, 32), pl.ds(col, width)
        ]

    for b in range(NB):
        col, width = BACK[b]
        part[1, :, col : col + width] = dot_nt(pre_grad[1], wi[col : col + width, :])
        back_across(b).start()
        part[0, :, col : col + width] = dot_nt(pre_grad[0], wi[col : col + width, :])
        if b > 0:
            back_ring(b - 1)
    back_ring(NB - 1)

    def back_plane(b):
        col, width = BACK[b]
        wait_bytes(back_in.at[pl.ds(0, 224), pl.ds(col, width)], bzr.at[b])
        back_send[:, col : col + width] = dot_nn(collect, back_in[:, col : col + width])

        def one(q, carry):
            there, device = plane_peer(q)
            remote(
                back_send.at[pl.ds(there * 8, 8), pl.ds(col, width)],
                sig.at[pl.ds(pos * 8, 8), pl.ds(col, width)],
                bps.at[b], bpr.at[b], device,
            ).start()
            return carry

        lax.fori_loop(1, PLANE, one, 0)
        sig[pl.ds(pos * 8, 8), pl.ds(col, width)] = back_send[
            pl.ds(pos * 8, 8), pl.ds(col, width)
        ]

    def arrived(b):
        col, width = BACK[b]
        wait_bytes(sig.at[pl.ds(0, 120), pl.ds(col, width)], bpr.at[b])
        grad = split(sig[:, col : col + width])
        tokens = (acts_s[0, :, col : col + width], acts_s[1, :, col : col + width])
        term = three(dot_nt, tokens, grad)
        if b == 0:
            disp_grad[...] = term
        else:
            disp_grad[...] += term
        dacts[:, col : col + width] = three(dot_nn, (disp_s[0], disp_s[1]), grad)

    for b in range(NB):
        back_plane(b)
        if b > 0:
            arrived(b - 1)
    arrived(NB - 1)

    dispatch = disp[...]
    grad = disp_grad[...]
    logit_grad = comb_term[...] + dispatch * (
        grad - jnp.sum(grad * dispatch, axis=0, keepdims=True)
    )
    grad_s = split(logit_grad)
    grad_t = split(logit_grad.T)
    for b in range(NB):
        col, width = BACK[b]
        dp[:, col : col + width] = three(
            dot_nn, grad_t, (acts_s[0, :, col : col + width], acts_s[1, :, col : col + width])
        )

    for k in range(2):
        remote(
            dp.at[:, pl.ds(pl.multiple_of(k * HALF + (1 - core) * 256, 128), 384)],
            dp_in.at[:, pl.ds(k * 384, 384)],
            dps.at[k], dpr.at[k], other,
        ).start()
    for b in range(NB):
        col, width = BACK[b]
        dacts[:, col : col + width] += three(
            dot_nt, grad_s, (sp_s[0, col : col + width, :], sp_s[1, col : col + width, :])
        )
    store = pltpu.make_async_copy(dacts, dacts_hbm, out_sem)
    store.start()
    for k in range(2):
        cols = pl.ds(pl.multiple_of(k * HALF + core * 256, 128), 384)
        wait_bytes(dp_in.at[:, pl.ds(k * 384, 384)], dpr.at[k])
        dp_sum[:, k * 384 : k * 384 + 384] = (
            dp[:, cols] + dp_in[:, k * 384 : k * 384 + 384]
        )

    def proj_plane(q, carry):
        there, device = plane_peer(q)
        remote(
            dp_sum.at[pl.ds(there * 8, 8)], dp_plane.at[pl.ds(pos * 8, 8)],
            dps.at[2], dpr.at[2], device,
        ).start()
        return carry

    lax.fori_loop(1, PLANE, proj_plane, 0)
    dp_plane[pl.ds(pos * 8, 8)] = dp_sum[pl.ds(pos * 8, 8)]
    wait_bytes(dp_plane.at[pl.ds(0, 120)], dpr.at[2])
    dp_ring[...] = jnp.sum(dp_plane[...].reshape(PLANE, 8, 768), axis=0)

    def proj_ring(q, carry):
        there, _, device = ring_peer(q)
        remote(
            dp_ring.at[:, pl.ds(pl.multiple_of(lax.div(there, 4) * 384, 128), 384)],
            dp_back.at[pl.ds(z * 8, 8)],
            dps.at[3], dpr.at[3], device,
        ).start()
        return carry

    lax.fori_loop(1, RING, proj_ring, 0)
    dp_back[pl.ds(z * 8, 8)] = dp_ring[:, pl.ds(pl.multiple_of(z_hi * 384, 128), 384)]
    wait_bytes(dp_back.at[pl.ds(0, 56)], dpr.at[3])
    total = jnp.sum(dp_back[...].reshape(RING, 8, 384), axis=0)
    mine = jnp.where(z_lo == 0, total[0:2], 0.0)
    for k in range(1, 4):
        mine = mine + jnp.where(z_lo == k, total[2 * k : 2 * k + 2], 0.0)
    dproj_ref[...] = jnp.where(core == 0, mine[:, 0:320], mine[:, 64:384])

    for k in range(NF):
        kind, col, width = FORWARD[k]
        wait_bytes(plane_in.at[kind, pl.ds(0, 240), pl.ds(col, width)], fps.at[k])
        wait_bytes(ring_in.at[kind, :, pl.ds(0, 224), pl.ds(col, width)], fzs.at[k])
        wait_bytes(ring_in.at[kind, :, :, pl.ds(col, width)], fcs.at[k])
    for b in range(NB):
        col, width = BACK[b]
        wait_bytes(part_in.at[:, pl.ds(col, width)], bcs.at[b])
        wait_bytes(back_in.at[pl.ds(0, 224), pl.ds(col, width)], bzs.at[b])
        wait_bytes(sig.at[pl.ds(0, 120), pl.ds(col, width)], bps.at[b])
    for k in range(2):
        wait_bytes(dp_in.at[:, pl.ds(k * 384, 384)], dps.at[k])
    wait_bytes(dp_plane.at[pl.ds(0, 120)], dps.at[2])
    wait_bytes(dp_back.at[pl.ds(0, 56)], dps.at[3])
    store.wait()


def local(activations, out_grad, slot_out, slot_proj, w_in, w_out):
    vmem = pltpu.VMEM
    sems = pltpu.SemaphoreType.DMA
    any_space = pl.BlockSpec(memory_space=pl.ANY)
    d_acts, d_proj = pl.pallas_call(
        kernel,
        out_shape=(
            jax.ShapeDtypeStruct((TOKENS, D), F32),
            jax.ShapeDtypeStruct((2, 320), F32),
        ),
        in_specs=[any_space] * 6,
        out_specs=(any_space, pl.BlockSpec(memory_space=pltpu.VMEM)),
        scratch_shapes=[
            vmem((TOKENS, D), F32),
            vmem((TOKENS, D), F32),
            vmem((SLOTS, D), F32),
            vmem((D, SLOTS), F32),
            vmem((D, D), BF16),
            vmem((D, D), BF16),
            vmem((2, TOKENS, D), BF16),
            vmem((2, TOKENS, D), BF16),
            vmem((2, SLOTS, D), BF16),
            vmem((2, D, SLOTS), BF16),
            vmem((2, TOKENS, SLOTS), BF16),
            vmem((TOKENS, SLOTS), F32),
            vmem((TOKENS, SLOTS), F32),
            vmem((TOKENS, SLOTS), F32),
            vmem((TOKENS, SLOTS), F32),
            vmem((TOKENS, D), F32),
            vmem((2, ROWS, HALF), BF16),
            vmem((2, ROWS, HALF), BF16),
            vmem((2, 8, 32, HALF), BF16),
            vmem((2, 2, ROWS, HALF), BF16),
            vmem((2, 2, ROWS, HALF), BF16),
            vmem((2, 2, ROWS, D), F32),
            vmem((2, ROWS, D), BF16),
            vmem((2, ROWS, D), F32),
            vmem((ROWS, D), F32),
            vmem((ROWS, D), BF16),
            vmem((ROWS, D), BF16),
            vmem((SLOTS, D), F32),
            vmem((SLOTS, D), F32),
            vmem((SLOTS, D), F32),
            vmem((SLOTS, 768), F32),
            vmem((SLOTS, 768), F32),
            vmem((SLOTS, 768), F32),
            vmem((8, 768), F32),
            vmem((64, 384), F32),
            sems((6,)),
            sems((NF,)), sems((NF,)), sems((NF,)), sems((NF,)), sems((NF,)), sems((NF,)),
            sems((NB,)), sems((NB,)), sems((NB,)), sems((NB,)), sems((NB,)), sems((NB,)),
            sems((4,)), sems((4,)),
            sems,
        ],
        compiler_params=pltpu.CompilerParams(
            collective_id=0, has_side_effects=True, vmem_limit_bytes=56 * 2**20
        ),
        name="soft_moe_backward",
    )(activations[0], out_grad[0], slot_out[0], slot_proj, w_in[0], w_out[0])
    return d_acts[None], d_proj.T


def solution(mesh):
    placed = (
        P(("ep", "tp"), None, None),
        P(("ep", "tp"), None, None),
        P(("ep", "tp"), None, None),
        P(),
        P("ep", None, "tp"),
        P("ep", "tp", None),
    )
    return jax.shard_map(
        local,
        mesh=mesh,
        in_specs=placed,
        out_specs=(P(("ep", "tp"), None, None), P("tp", "ep")),
        check_vma=False,
    )
```

```python
import functools

import jax
import jax.numpy as jnp
from jax import lax
from jax.experimental import pallas as pl
from jax.experimental.pallas import tpu as pltpu
from jax.sharding import PartitionSpec as P

MESH = pl.DeviceIdType.MESH
F32 = jnp.float32
BF16 = jnp.bfloat16
D = 1280
HALF = 640
TOKENS = 256
SLOTS = 128
ROWS = 256
PLANE = 16
RING = 8
WIDE = 256
FORWARD = (
    (0, 0, 256), (0, 256, 256), (0, 512, 128),
    (1, 0, 256), (1, 256, 256), (1, 512, 128),
)
BACK = ((0, 256), (256, 256), (512, 128))
NF, NB = len(FORWARD), len(BACK)


def gelu_slope(pre_act):
    normal_cdf = 0.5 * (1.0 + lax.erf(pre_act * 0.7071067811865476))
    density = jnp.exp(-0.5 * pre_act * pre_act) * 0.3989422804014327
    return normal_cdf + pre_act * density


def dot_nn(a, b):
    return jnp.dot(a, b, preferred_element_type=F32)


def dot_nt(a, b):
    return lax.dot_general(a, b, (((1,), (1,)), ((), ())), preferred_element_type=F32)


def split(a):
    high = a.astype(BF16)
    return high, (a - high.astype(F32)).astype(BF16)


def three(dot, a, b):
    return dot(a[0], b[0]) + (dot(a[0], b[1]) + dot(a[1], b[0]))


def iota2(shape, axis):
    return lax.broadcasted_iota(jnp.int32, shape, axis)


def one_hot(condition):
    return jnp.where(condition, 1.0, 0.0).astype(BF16)


def kernel(
    acts_hbm, og_hbm, so_hbm, sp_hbm, wi_hbm, wo_hbm,
    dacts_hbm, dproj_ref,
    acts, og, so, sp, wi, wo,
    acts_s, og_s, so_s, sp_s, disp_s, disp, comb, comb_term, disp_grad, logit_grad, dacts,
    slots, send, plane_in, ring_out, ring_in, first_out, first_in, first_send, first_plane,
    acc, pre_grad, part, part_in, back_out, back_in, back_send, sig,
    dp_out, dp_own, dp_in, dp_sum, dp_plane, dp_ring, dp_back,
    load_sem, fps, fpr, fzs, fzr, fcs, fcr, bcs, bcr, bzs, bzr, bps, bpr, dps, dpr, out_sem,
):
    ep, tp = lax.axis_index("ep"), lax.axis_index("tp")
    z_lo, pos = lax.div(ep, 16), lax.rem(ep, 16)
    x, y = lax.div(pos, 4), lax.rem(pos, 4)
    z_hi, core = lax.div(tp, 2), lax.rem(tp, 2)
    z = z_hi * 4 + z_lo
    other = {"ep": ep, "tp": z_hi * 2 + (1 - core)}

    def plane_peer(q):
        there = lax.rem(x + lax.div(q, 4), 4) * 4 + lax.rem(y + lax.rem(q, 4), 4)
        return there, {"ep": z_lo * 16 + there, "tp": tp}

    def ring_peer(q):
        there = lax.rem(z + q, RING)
        lo = lax.rem(there, 4)
        return there, lo, {"ep": lo * 16 + pos, "tp": lax.div(there, 4) * 2 + core}

    def remote(src, dst, send_sem, recv_sem, device):
        return pltpu.make_async_remote_copy(
            src_ref=src, dst_ref=dst, send_sem=send_sem, recv_sem=recv_sem,
            device_id=device, device_id_type=MESH,
        )

    def wait_bytes(ref, sem):
        pltpu.make_async_copy(ref, ref, sem).wait()

    loads = []
    pairs = ((sp_hbm, sp), (acts_hbm, acts), (og_hbm, og), (so_hbm, so), (wi_hbm, wi), (wo_hbm, wo))
    for k, (src, dst) in enumerate(pairs):
        loads.append(pltpu.make_async_copy(src, dst, load_sem.at[k]))
        loads[-1].start()
    load_sp, load_acts, load_og, load_so, load_wi, load_wo = loads

    barrier = pltpu.get_barrier_semaphore()

    def greet_plane(q, carry):
        pl.semaphore_signal(barrier, inc=1, device_id=plane_peer(q)[1], device_id_type=MESH)
        return carry

    def greet_ring(q, carry):
        pl.semaphore_signal(barrier, inc=1, device_id=ring_peer(q)[2], device_id_type=MESH)
        return carry

    lax.fori_loop(1, PLANE, greet_plane, 0)
    lax.fori_loop(1, RING, greet_ring, 0)
    pl.semaphore_signal(barrier, inc=1, device_id=other, device_id_type=MESH)

    n, r = iota2((SLOTS, SLOTS), 0), iota2((SLOTS, SLOTS), 1)
    to_order = one_hot(n == lax.rem(r, 4) * 32 + lax.rem(lax.div(r, 4), 16) * 2 + lax.div(r, 64))
    to_order_t = one_hot(r == lax.rem(n, 4) * 32 + lax.rem(lax.div(n, 4), 16) * 2 + lax.div(n, 64))
    o, i = iota2((ROWS, ROWS), 0), iota2((ROWS, ROWS), 1)
    spread = one_hot(
        i == lax.rem(lax.div(o, 4), 4) * 64 + lax.div(o, 16) * 4 + lax.rem(o, 4)
    )
    regroup = one_hot(
        i == lax.rem(o, 16) * 16 + lax.rem(lax.div(o, 16), 4) * 4 + lax.div(o, 64)
    )
    direct = one_hot(
        i == lax.rem(lax.div(o, 16), 4) * 64 + lax.rem(o, 16) * 4 + lax.div(o, 64)
    )
    to_plane = one_hot(
        i == lax.rem(lax.div(o, 8), 2) * 128 + lax.rem(o, 8) * 16 + lax.div(o, 16)
    )
    from_plane = one_hot(
        o == lax.rem(lax.div(i, 8), 2) * 128 + lax.rem(i, 8) * 16 + lax.div(i, 16)
    )
    o, i = iota2((SLOTS, ROWS), 0), iota2((SLOTS, ROWS), 1)
    collect = one_hot(
        (lax.div(i, 128) == lax.rem(lax.div(o, 4), 2))
        & (lax.rem(i, 64) == lax.rem(o, 4) * 16 + lax.div(o, 8))
    )
    def place(s, h):
        return one_hot(
            (lax.div(n, 64) == s)
            & (r == lax.div(lax.rem(n, 64), 4) * 8 + h * 4 + lax.rem(n, 4))
        )

    def twice(s):
        return one_hot(r == s * 64 + lax.div(n, 8) * 4 + lax.rem(n, 4))

    load_sp.wait()
    for k, part_of in enumerate(split(sp[...])):
        sp_s[k] = dot_nn(part_of, to_order).astype(BF16)
    load_acts.wait()
    acts_s[0], acts_s[1] = split(acts[...])
    logits = three(dot_nn, (acts_s[0], acts_s[1]), (sp_s[0], sp_s[1]))
    e = jnp.exp(logits - jnp.max(logits, axis=0, keepdims=True))
    dispatch = e / jnp.sum(e, axis=0, keepdims=True)
    disp[...] = dispatch
    disp_s[0], disp_s[1] = split(dispatch)
    dispatch_t = split(dispatch.T)
    e = jnp.exp(logits - jnp.max(logits, axis=1, keepdims=True))
    combine = e / jnp.sum(e, axis=1, keepdims=True)
    comb[...] = combine
    combine_t = split(combine.T)
    load_og.wait()
    og_s[0], og_s[1] = split(og[...])

    def slot_rows(col, width):
        for kind, weights_t, values in ((0, dispatch_t, acts_s), (1, combine_t, og_s)):
            for h in range(2):
                c = h * HALF + col
                rows = three(
                    dot_nn, weights_t, (values[0, :, c : c + width], values[1, :, c : c + width])
                )
                slots[kind, :, c : c + width] = rows.astype(BF16)

    def across(k):
        s, col, width = FORWARD[k]
        return remote(
            ring_in.at[s, :, pl.ds(0, 128), pl.ds(col, width)],
            ring_in.at[s, :, pl.ds(128, 128), pl.ds(col, width)],
            fcs.at[k], fcr.at[k], other,
        )

    def stacked(k):
        s, col, width = FORWARD[k]
        parts = [
            slots[kind, s * 64 : s * 64 + 64, h * HALF + col : h * HALF + col + width]
            for h in range(2) for kind in range(2)
        ]
        return jnp.concatenate(parts, axis=0)

    def first_ring():
        rows = dot_nn(direct, stacked(0)).astype(BF16)
        first_out[...] = rows.reshape(16, 16, WIDE)
        pl.semaphore_wait(barrier, PLANE - 1 + RING - 1 + 1)

        def one(q, carry):
            there, lo, device = ring_peer(q)
            remote(
                first_out.at[pl.ds(lo * 4, 4)],
                first_in.at[:, pl.ds(z * 16, 16)],
                fzs.at[0], fzr.at[0], device,
            ).start()
            return carry

        lax.fori_loop(1, RING, one, 0)
        first_in[:, pl.ds(z * 16, 16)] = first_out[pl.ds(z_lo * 4, 4)]

    def first_spread():
        wait_bytes(first_in.at[:, pl.ds(0, 112)], fzr.at[0])
        for h in range(2):
            rows = first_in[2 * h : 2 * h + 2].reshape(ROWS, WIDE)
            first_send[h] = dot_nn(to_plane, rows).astype(BF16)

        def one(q, carry):
            there, device = plane_peer(q)
            remote(
                first_send.at[:, pl.ds(there * 16, 16)],
                first_plane.at[:, pl.ds(pos * 16, 16)],
                fps.at[0], fpr.at[0], device,
            ).start()
            return carry

        lax.fori_loop(1, PLANE, one, 0)
        first_plane[:, pl.ds(pos * 16, 16)] = first_send[:, pl.ds(pos * 16, 16)]

    def first_arrived():
        wait_bytes(first_plane.at[:, pl.ds(0, 240)], fpr.at[0])
        for h in range(2):
            rows = dot_nn(from_plane, first_plane[h]).astype(BF16)
            ring_in[0, 2 * h : 2 * h + 2, 0:128, 0:WIDE] = rows.reshape(2, 128, WIDE)
        across(0).start()

    def plane_send(k):
        s, col, width = FORWARD[k]
        send[s, :, col : col + width] = dot_nn(spread, stacked(k)).astype(BF16)

        def one(q, carry):
            there, device = plane_peer(q)
            remote(
                send.at[s, pl.ds(there * 16, 16), pl.ds(col, width)],
                plane_in.at[s, pl.ds(pos * 16, 16), pl.ds(col, width)],
                fps.at[k], fpr.at[k], device,
            ).start()
            return carry

        lax.fori_loop(1, PLANE, one, 0)
        plane_in[s, pl.ds(pos * 16, 16), pl.ds(col, width)] = send[
            s, pl.ds(pos * 16, 16), pl.ds(col, width)
        ]

    slot_rows(FORWARD[0][1], FORWARD[0][2])
    first_ring()
    for k in range(1, NF // 2):
        slot_rows(FORWARD[k][1], FORWARD[k][2])
        plane_send(k)
    for k in range(NF // 2, NF):
        plane_send(k)

    def ring_send(k):
        s, col, width = FORWARD[k]
        wait_bytes(plane_in.at[s, pl.ds(0, 240), pl.ds(col, width)], fpr.at[k])
        moved = dot_nn(regroup, plane_in[s, :, col : col + width])
        ring_out[s, :, :, col : col + width] = moved.astype(BF16).reshape(16, 16, width)

        def one(q, carry):
            there, lo, device = ring_peer(q)
            remote(
                ring_out.at[s, pl.ds(lo * 4, 4), :, pl.ds(col, width)],
                ring_in.at[s, :, pl.ds(z * 16, 16), pl.ds(col, width)],
                fzs.at[k], fzr.at[k], device,
            ).start()
            return carry

        lax.fori_loop(1, RING, one, 0)
        ring_in[s, :, pl.ds(z * 16, 16), pl.ds(col, width)] = ring_out[
            s, pl.ds(z_lo * 4, 4), :, pl.ds(col, width)
        ]

    ring_send(1)
    ring_send(2)
    first_spread()
    for k in range(NF // 2, NF):
        ring_send(k)

    load_so.wait()
    for k, part_of in enumerate(split(so[...])):
        so_s[k] = dot_nn(to_order_t, part_of).astype(BF16)
    comb_grad = three(dot_nt, (og_s[0], og_s[1]), (so_s[0], so_s[1]))
    combine = comb[...]
    comb_term[...] = combine * (
        comb_grad - jnp.sum(comb_grad * combine, axis=1, keepdims=True)
    )

    load_wi.wait()
    load_wo.wait()

    def ring_arrived(k):
        s, col, width = FORWARD[k]
        wait_bytes(ring_in.at[s, :, pl.ds(0, 112), pl.ds(col, width)], fzr.at[k])
        across(k).start()

    def expert(k):
        s, col, width = FORWARD[k]
        across(k).wait_recv()

        def tile(t, carry):
            c = pl.multiple_of(t * 256, 256)
            first, second = None, None
            for h in range(2):
                d = h * HALF + col
                rows_in = ring_in[s, 2 * h, :, col : col + width]
                rows_grad = ring_in[s, 2 * h + 1, :, col : col + width]
                one = dot_nn(rows_in, wi[pl.ds(d, width), pl.ds(c, 256)])
                two = dot_nt(rows_grad, wo[pl.ds(c, 256), pl.ds(d, width)])
                first = one if first is None else first + one
                second = two if second is None else second + two
            if col > 0:
                first = first + acc[0, s, :, pl.ds(c, 256)]
                second = second + acc[1, s, :, pl.ds(c, 256)]
            if col + width == HALF:
                pre_grad[s, :, pl.ds(c, 256)] = (second * gelu_slope(first)).astype(BF16)
            else:
                acc[0, s, :, pl.ds(c, 256)] = first
                acc[1, s, :, pl.ds(c, 256)] = second
            return carry

        lax.fori_loop(0, 5, tile, 0)

    def back_across(s, b):
        col, width = BACK[b]
        return remote(
            part.at[s, :, pl.ds(128, 128), pl.ds(col, width)],
            part_in.at[s, :, :, pl.ds(col, width)],
            bcs.at[s, b], bcr.at[s, b], other,
        )

    def expert_back(s, b):
        col, width = BACK[b]
        for h in range(2):
            part[s, h, :, col : col + width] = dot_nt(
                pre_grad[s], wi[h * HALF + col : h * HALF + col + width, :]
            )
        back_across(s, b).start()

    def back_ring(s, b):
        col, width = BACK[b]
        back_across(s, b).wait_recv()
        both = part[s, :, 0:128, col : col + width] + part_in[s, :, :, col : col + width]
        back_out[s, :, :, col : col + width] = both.astype(BF16)

        def one(q, carry):
            there, _, device = ring_peer(q)
            remote(
                back_out.at[s, :, pl.ds(there * 16, 16), pl.ds(col, width)],
                back_in.at[s, :, pl.ds(z * 16, 16), pl.ds(col, width)],
                bzs.at[s, b], bzr.at[s, b], device,
            ).start()
            return carry

        lax.fori_loop(1, RING, one, 0)
        back_in[s, :, pl.ds(z * 16, 16), pl.ds(col, width)] = back_out[
            s, :, pl.ds(z * 16, 16), pl.ds(col, width)
        ]

    def back_plane(s, b):
        col, width = BACK[b]
        wait_bytes(back_in.at[s, :, pl.ds(0, 112), pl.ds(col, width)], bzr.at[s, b])
        back_send[s, :, col : col + width] = dot_nn(
            collect, back_in[s, :, :, col : col + width].reshape(ROWS, width)
        )

        def one(q, carry):
            there, device = plane_peer(q)
            remote(
                back_send.at[s, pl.ds(there * 8, 8), pl.ds(col, width)],
                sig.at[s, pl.ds(pos * 8, 8), pl.ds(col, width)],
                bps.at[s, b], bpr.at[s, b], device,
            ).start()
            return carry

        lax.fori_loop(1, PLANE, one, 0)
        sig[s, pl.ds(pos * 8, 8), pl.ds(col, width)] = back_send[
            s, pl.ds(pos * 8, 8), pl.ds(col, width)
        ]

    def arrived(s, b):
        col, width = BACK[b]
        wait_bytes(sig.at[s, pl.ds(0, 120), pl.ds(col, width)], bpr.at[s, b])
        high, low = split(sig[s, :, col : col + width])
        for h in range(2):
            c = h * HALF + col
            there = place(s, h)
            grad = (dot_nn(there, high).astype(BF16), dot_nn(there, low).astype(BF16))
            tokens = (acts_s[0, :, c : c + width], acts_s[1, :, c : c + width])
            term = three(dot_nt, tokens, grad)
            if s == 0 and b == 0 and h == 0:
                disp_grad[...] = term
            else:
                disp_grad[...] += term
            term = three(dot_nn, (disp_s[0], disp_s[1]), grad)
            if s == 0:
                dacts[:, c : c + width] = term
            else:
                dacts[:, c : c + width] += term

    def proj_across(s):
        return remote(dp_out.at[s], dp_in.at[s], dps.at[s, 0], dpr.at[s, 0], other)

    def proj_start(s):
        dispatch = disp[...]
        grad = disp_grad[...]
        whole = comb_term[...] + dispatch * (
            grad - jnp.sum(grad * dispatch, axis=0, keepdims=True)
        )
        logit_grad[...] = whole
        rows = [dot_nn(twice(s), a).astype(BF16) for a in split(whole.T)]
        upper = lax.rem(lax.div(iota2((SLOTS, 384), 0), 4), 2) == 0

        def half(which):
            terms = []
            for k in range(2):
                cols = pl.ds(pl.multiple_of(k * HALF + which * 256, 128), 384)
                terms.append(three(dot_nn, rows, (acts_s[0, :, cols], acts_s[1, :, cols])))
            return jnp.where(upper, terms[0], terms[1])

        dp_out[s] = half(1 - core)
        proj_across(s).start()
        dp_own[s] = half(core)

    def proj_plane(s):
        proj_across(s).wait_recv()
        dp_sum[s] = dp_own[s] + dp_in[s]

        def one(q, carry):
            there, device = plane_peer(q)
            remote(
                dp_sum.at[s, pl.ds(there * 8, 8)], dp_plane.at[s, pl.ds(pos * 8, 8)],
                dps.at[s, 1], dpr.at[s, 1], device,
            ).start()
            return carry

        lax.fori_loop(1, PLANE, one, 0)
        dp_plane[s, pl.ds(pos * 8, 8)] = dp_sum[s, pl.ds(pos * 8, 8)]

    def proj_ring(s):
        wait_bytes(dp_plane.at[s, pl.ds(0, 120)], dpr.at[s, 1])
        dp_ring[s] = jnp.sum(dp_plane[s].reshape(PLANE, 8, 384), axis=0)

        def one(q, carry):
            there, _, device = ring_peer(q)
            remote(
                dp_ring.at[s], dp_back.at[s, pl.ds(z * 8, 8)],
                dps.at[s, 2], dpr.at[s, 2], device,
            ).start()
            return carry

        lax.fori_loop(1, RING, one, 0)
        dp_back[s, pl.ds(z * 8, 8)] = dp_ring[s]

    def proj_end(s):
        wait_bytes(dp_back.at[s, pl.ds(0, 56)], dpr.at[s, 2])
        total = jnp.sum(dp_back[s].reshape(RING, 8, 384), axis=0)
        mine = jnp.sum(
            jnp.where(iota2((8, 384), 0) == z, total, 0.0), axis=0, keepdims=True
        )
        dproj_ref[s : s + 1, :] = jnp.where(core == 0, mine[:, 0:320], mine[:, 64:384])

    first_arrived()
    expert(0)
    for k in range(1, NF // 2):
        ring_arrived(k)
        expert(k)
    for b in range(NB):
        expert_back(0, b)
    ring_arrived(3)
    expert(3)
    ring_arrived(4)
    for b in range(NB):
        back_ring(0, b)
    expert(4)
    ring_arrived(5)
    expert(5)
    for b in range(NB):
        expert_back(1, b)
        if b > 0:
            back_ring(1, b - 1)
    back_ring(1, NB - 1)
    for s in range(2):
        for b in range(NB):
            back_plane(s, b)
    for b in range(NB):
        arrived(0, b)
    proj_start(0)
    proj_plane(0)
    for b in range(NB):
        arrived(1, b)
    proj_start(1)
    proj_ring(0)
    proj_plane(1)
    whole = split(logit_grad[...])
    for c in range(0, D, 256):
        dacts[:, c : c + 256] += three(
            dot_nt, whole, (sp_s[0, c : c + 256, :], sp_s[1, c : c + 256, :])
        )
    store = pltpu.make_async_copy(dacts, dacts_hbm, out_sem)
    store.start()
    proj_ring(1)
    proj_end(0)
    proj_end(1)

    for k in range(NF):
        s, col, width = FORWARD[k]
        if k == 0:
            wait_bytes(first_plane.at[:, pl.ds(0, 240)], fps.at[k])
            wait_bytes(first_in.at[:, pl.ds(0, 112)], fzs.at[k])
        else:
            wait_bytes(plane_in.at[s, pl.ds(0, 240), pl.ds(col, width)], fps.at[k])
            wait_bytes(ring_in.at[s, :, pl.ds(0, 112), pl.ds(col, width)], fzs.at[k])
        across(k).wait_send()
    for s in range(2):
        for b in range(NB):
            col, width = BACK[b]
            back_across(s, b).wait_send()
            wait_bytes(back_in.at[s, :, pl.ds(0, 112), pl.ds(col, width)], bzs.at[s, b])
            wait_bytes(sig.at[s, pl.ds(0, 120), pl.ds(col, width)], bps.at[s, b])
        proj_across(s).wait_send()
        wait_bytes(dp_plane.at[s, pl.ds(0, 120)], dps.at[s, 1])
        wait_bytes(dp_back.at[s, pl.ds(0, 56)], dps.at[s, 2])
    store.wait()


def local(activations, out_grad, slot_out, slot_proj, w_in, w_out):
    vmem = pltpu.VMEM
    sems = pltpu.SemaphoreType.DMA
    any_space = pl.BlockSpec(memory_space=pl.ANY)
    d_acts, d_proj = pl.pallas_call(
        kernel,
        out_shape=(
            jax.ShapeDtypeStruct((TOKENS, D), F32),
            jax.ShapeDtypeStruct((2, 320), F32),
        ),
        in_specs=[any_space] * 6,
        out_specs=(any_space, pl.BlockSpec(memory_space=pltpu.VMEM)),
        scratch_shapes=[
            vmem((TOKENS, D), F32),
            vmem((TOKENS, D), F32),
            vmem((SLOTS, D), F32),
            vmem((D, SLOTS), F32),
            vmem((D, D), BF16),
            vmem((D, D), BF16),
            vmem((2, TOKENS, D), BF16),
            vmem((2, TOKENS, D), BF16),
            vmem((2, SLOTS, D), BF16),
            vmem((2, D, SLOTS), BF16),
            vmem((2, TOKENS, SLOTS), BF16),
            vmem((TOKENS, SLOTS), F32),
            vmem((TOKENS, SLOTS), F32),
            vmem((TOKENS, SLOTS), F32),
            vmem((TOKENS, SLOTS), F32),
            vmem((TOKENS, SLOTS), F32),
            vmem((TOKENS, D), F32),
            vmem((2, SLOTS, D), BF16),
            vmem((2, ROWS, HALF), BF16),
            vmem((2, ROWS, HALF), BF16),
            vmem((2, 16, 16, HALF), BF16),
            vmem((2, 4, ROWS, HALF), BF16),
            vmem((16, 16, WIDE), BF16),
            vmem((4, 128, WIDE), BF16),
            vmem((2, ROWS, WIDE), BF16),
            vmem((2, ROWS, WIDE), BF16),
            vmem((2, 2, ROWS, D), F32),
            vmem((2, ROWS, D), BF16),
            vmem((2, 2, ROWS, HALF), F32),
            vmem((2, 2, 128, HALF), F32),
            vmem((2, 2, 128, HALF), BF16),
            vmem((2, 2, 128, HALF), BF16),
            vmem((2, SLOTS, HALF), F32),
            vmem((2, SLOTS, HALF), F32),
            vmem((2, SLOTS, 384), F32),
            vmem((2, SLOTS, 384), F32),
            vmem((2, SLOTS, 384), F32),
            vmem((2, SLOTS, 384), F32),
            vmem((2, SLOTS, 384), F32),
            vmem((2, 8, 384), F32),
            vmem((2, 64, 384), F32),
            sems((6,)),
            sems((NF,)), sems((NF,)), sems((NF,)), sems((NF,)), sems((NF,)), sems((NF,)),
            sems((2, NB)), sems((2, NB)), sems((2, NB)), sems((2, NB)), sems((2, NB)), sems((2, NB)),
            sems((2, 3)), sems((2, 3)),
            sems,
        ],
        compiler_params=pltpu.CompilerParams(
            collective_id=0, has_side_effects=True, vmem_limit_bytes=56 * 2**20
        ),
        name="soft_moe_backward",
    )(activations[0], out_grad[0], slot_out[0], slot_proj, w_in[0], w_out[0])
    return d_acts[None], d_proj.T


def solution(mesh):
    placed = (
        P(("ep", "tp"), None, None),
        P(("ep", "tp"), None, None),
        P(("ep", "tp"), None, None),
        P(),
        P("ep", None, "tp"),
        P("ep", "tp", None),
    )
    return jax.shard_map(
        local,
        mesh=mesh,
        in_specs=placed,
        out_specs=(P(("ep", "tp"), None, None), P("tp", "ep")),
        check_vma=False,
    )
```

```python
import functools

import jax
import jax.numpy as jnp
from jax import lax
from jax.experimental import pallas as pl
from jax.experimental.pallas import tpu as pltpu
from jax.sharding import PartitionSpec as P

MESH = pl.DeviceIdType.MESH
F32 = jnp.float32
BF16 = jnp.bfloat16
D = 1280
HALF = 640
TOKENS = 256
SLOTS = 128
ROWS = 256
PLANE = 16
RING = 8
WIDE = 256
FORWARD = (
    (0, 0, 256), (0, 256, 256), (0, 512, 128),
    (1, 0, 256), (1, 256, 256), (1, 512, 128),
)
BACK = ((0, 256), (256, 256), (512, 128))
NF, NB = len(FORWARD), len(BACK)


def gelu_slope(pre_act):
    normal_cdf = 0.5 * (1.0 + lax.erf(pre_act * 0.7071067811865476))
    density = jnp.exp(-0.5 * pre_act * pre_act) * 0.3989422804014327
    return normal_cdf + pre_act * density


def dot_nn(a, b):
    return jnp.dot(a, b, preferred_element_type=F32)


def dot_nt(a, b):
    return lax.dot_general(a, b, (((1,), (1,)), ((), ())), preferred_element_type=F32)


def split(a):
    high = a.astype(BF16)
    return high, (a - high.astype(F32)).astype(BF16)


def three(dot, a, b):
    return dot(a[0], b[0]) + (dot(a[0], b[1]) + dot(a[1], b[0]))


def iota2(shape, axis):
    return lax.broadcasted_iota(jnp.int32, shape, axis)


def one_hot(condition):
    return jnp.where(condition, 1.0, 0.0).astype(BF16)


def kernel(
    acts_hbm, og_hbm, so_hbm, sp_hbm, wi_hbm, wo_hbm,
    dacts, dproj_ref,
    acts, og, so, sp, wi, wo,
    acts_s, og_s, so_s, sp_s, disp_s, disp, comb, comb_term, disp_grad, logit_grad, grad_s,
    slots, send, plane_in, ring_out, ring_in, first_out, first_in, first_send, first_plane,
    acc, pre_grad, part, part_in, back_out, back_in, back_send, sig,
    dp_out, dp_own, dp_in, dp_sum, dp_plane, dp_ring, dp_back,
    load_sem, fps, fpr, fzs, fzr, fcs, fcr, bcs, bcr, bzs, bzr, bps, bpr, dps, dpr,
):
    ep, tp = lax.axis_index("ep"), lax.axis_index("tp")
    z_lo, pos = lax.div(ep, 16), lax.rem(ep, 16)
    x, y = lax.div(pos, 4), lax.rem(pos, 4)
    z_hi, core = lax.div(tp, 2), lax.rem(tp, 2)
    z = z_hi * 4 + z_lo
    other = {"ep": ep, "tp": z_hi * 2 + (1 - core)}

    def plane_peer(q):
        there = lax.rem(x + lax.div(q, 4), 4) * 4 + lax.rem(y + lax.rem(q, 4), 4)
        return there, {"ep": z_lo * 16 + there, "tp": tp}

    def ring_peer(q):
        there = lax.rem(z + q, RING)
        lo = lax.rem(there, 4)
        return there, lo, {"ep": lo * 16 + pos, "tp": lax.div(there, 4) * 2 + core}

    def remote(src, dst, send_sem, recv_sem, device):
        return pltpu.make_async_remote_copy(
            src_ref=src, dst_ref=dst, send_sem=send_sem, recv_sem=recv_sem,
            device_id=device, device_id_type=MESH,
        )

    def wait_bytes(ref, sem):
        pltpu.make_async_copy(ref, ref, sem).wait()

    loads = []
    pairs = ((sp_hbm, sp), (acts_hbm, acts), (og_hbm, og), (so_hbm, so), (wi_hbm, wi), (wo_hbm, wo))
    for k, (src, dst) in enumerate(pairs):
        loads.append(pltpu.make_async_copy(src, dst, load_sem.at[k]))
        loads[-1].start()
    load_sp, load_acts, load_og, load_so, load_wi, load_wo = loads

    barrier = pltpu.get_barrier_semaphore()

    def greet_plane(q, carry):
        pl.semaphore_signal(barrier, inc=1, device_id=plane_peer(q)[1], device_id_type=MESH)
        return carry

    def greet_ring(q, carry):
        pl.semaphore_signal(barrier, inc=1, device_id=ring_peer(q)[2], device_id_type=MESH)
        return carry

    lax.fori_loop(1, PLANE, greet_plane, 0)
    lax.fori_loop(1, RING, greet_ring, 0)
    pl.semaphore_signal(barrier, inc=1, device_id=other, device_id_type=MESH)

    n, r = iota2((SLOTS, SLOTS), 0), iota2((SLOTS, SLOTS), 1)
    to_order = one_hot(n == lax.rem(r, 4) * 32 + lax.rem(lax.div(r, 4), 16) * 2 + lax.div(r, 64))
    to_order_t = one_hot(r == lax.rem(n, 4) * 32 + lax.rem(lax.div(n, 4), 16) * 2 + lax.div(n, 64))
    o, i = iota2((ROWS, ROWS), 0), iota2((ROWS, ROWS), 1)
    spread = one_hot(
        i == lax.rem(lax.div(o, 4), 4) * 64 + lax.div(o, 16) * 4 + lax.rem(o, 4)
    )
    regroup = one_hot(
        i == lax.rem(o, 16) * 16 + lax.rem(lax.div(o, 16), 4) * 4 + lax.div(o, 64)
    )
    direct = one_hot(
        i == lax.rem(lax.div(o, 16), 4) * 64 + lax.rem(o, 16) * 4 + lax.div(o, 64)
    )
    to_plane = one_hot(
        i == lax.rem(lax.div(o, 8), 2) * 128 + lax.rem(o, 8) * 16 + lax.div(o, 16)
    )
    from_plane = one_hot(
        o == lax.rem(lax.div(i, 8), 2) * 128 + lax.rem(i, 8) * 16 + lax.div(i, 16)
    )
    o, i = iota2((SLOTS, ROWS), 0), iota2((SLOTS, ROWS), 1)
    collect = one_hot(
        (lax.div(i, 128) == lax.rem(lax.div(o, 4), 2))
        & (lax.rem(i, 64) == lax.rem(o, 4) * 16 + lax.div(o, 8))
    )
    def place(s, h):
        return one_hot(
            (lax.div(n, 64) == s)
            & (r == lax.div(lax.rem(n, 64), 4) * 8 + h * 4 + lax.rem(n, 4))
        )

    def twice(s):
        return one_hot(r == s * 64 + lax.div(n, 8) * 4 + lax.rem(n, 4))

    load_sp.wait()
    for k, part_of in enumerate(split(sp[...])):
        sp_s[k] = dot_nn(part_of, to_order).astype(BF16)
    load_acts.wait()
    acts_s[0], acts_s[1] = split(acts[...])
    logits = three(dot_nn, (acts_s[0], acts_s[1]), (sp_s[0], sp_s[1]))
    e = jnp.exp(logits - jnp.max(logits, axis=0, keepdims=True))
    dispatch = e / jnp.sum(e, axis=0, keepdims=True)
    disp[...] = dispatch
    disp_s[0], disp_s[1] = split(dispatch)
    dispatch_t = split(dispatch.T)
    e = jnp.exp(logits - jnp.max(logits, axis=1, keepdims=True))
    combine = e / jnp.sum(e, axis=1, keepdims=True)
    comb[...] = combine
    combine_t = split(combine.T)
    load_og.wait()

    def slot_rows(col, width):
        for h in range(2):
            c = h * HALF + col
            og_s[0, :, c : c + width], og_s[1, :, c : c + width] = split(og[:, c : c + width])
        for kind, weights_t, values in ((0, dispatch_t, acts_s), (1, combine_t, og_s)):
            for h in range(2):
                c = h * HALF + col
                rows = three(
                    dot_nn, weights_t, (values[0, :, c : c + width], values[1, :, c : c + width])
                )
                slots[kind, :, c : c + width] = rows.astype(BF16)

    def across(k):
        s, col, width = FORWARD[k]
        return remote(
            ring_in.at[s, :, pl.ds(0, 128), pl.ds(col, width)],
            ring_in.at[s, :, pl.ds(128, 128), pl.ds(col, width)],
            fcs.at[k], fcr.at[k], other,
        )

    def stacked(k):
        s, col, width = FORWARD[k]
        parts = [
            slots[kind, s * 64 : s * 64 + 64, h * HALF + col : h * HALF + col + width]
            for h in range(2) for kind in range(2)
        ]
        return jnp.concatenate(parts, axis=0)

    def first_ring():
        rows = dot_nn(direct, stacked(0)).astype(BF16)
        first_out[...] = rows.reshape(16, 16, WIDE)
        pl.semaphore_wait(barrier, PLANE - 1 + RING - 1 + 1)

        def one(q, carry):
            there, lo, device = ring_peer(q)
            remote(
                first_out.at[pl.ds(lo * 4, 4)],
                first_in.at[:, pl.ds(z * 16, 16)],
                fzs.at[0], fzr.at[0], device,
            ).start()
            return carry

        lax.fori_loop(1, RING, one, 0)
        first_in[:, pl.ds(z * 16, 16)] = first_out[pl.ds(z_lo * 4, 4)]

    def first_spread():
        wait_bytes(first_in.at[:, pl.ds(0, 112)], fzr.at[0])
        for h in range(2):
            rows = first_in[2 * h : 2 * h + 2].reshape(ROWS, WIDE)
            first_send[h] = dot_nn(to_plane, rows).astype(BF16)

        def one(q, carry):
            there, device = plane_peer(q)
            remote(
                first_send.at[:, pl.ds(there * 16, 16)],
                first_plane.at[:, pl.ds(pos * 16, 16)],
                fps.at[0], fpr.at[0], device,
            ).start()
            return carry

        lax.fori_loop(1, PLANE, one, 0)
        first_plane[:, pl.ds(pos * 16, 16)] = first_send[:, pl.ds(pos * 16, 16)]

    def first_arrived():
        wait_bytes(first_plane.at[:, pl.ds(0, 240)], fpr.at[0])
        for h in range(2):
            rows = dot_nn(from_plane, first_plane[h]).astype(BF16)
            ring_in[0, 2 * h : 2 * h + 2, 0:128, 0:WIDE] = rows.reshape(2, 128, WIDE)
        across(0).start()

    def plane_send(k):
        s, col, width = FORWARD[k]
        send[s, :, col : col + width] = dot_nn(spread, stacked(k)).astype(BF16)

        def one(q, carry):
            there, device = plane_peer(q)
            remote(
                send.at[s, pl.ds(there * 16, 16), pl.ds(col, width)],
                plane_in.at[s, pl.ds(pos * 16, 16), pl.ds(col, width)],
                fps.at[k], fpr.at[k], device,
            ).start()
            return carry

        lax.fori_loop(1, PLANE, one, 0)
        plane_in[s, pl.ds(pos * 16, 16), pl.ds(col, width)] = send[
            s, pl.ds(pos * 16, 16), pl.ds(col, width)
        ]

    slot_rows(FORWARD[0][1], FORWARD[0][2])
    first_ring()
    for k in range(1, NF // 2):
        slot_rows(FORWARD[k][1], FORWARD[k][2])
        plane_send(k)
    for k in range(NF // 2, NF):
        plane_send(k)

    def ring_send(k):
        s, col, width = FORWARD[k]
        wait_bytes(plane_in.at[s, pl.ds(0, 240), pl.ds(col, width)], fpr.at[k])
        moved = dot_nn(regroup, plane_in[s, :, col : col + width])
        ring_out[s, :, :, col : col + width] = moved.astype(BF16).reshape(16, 16, width)

        def one(q, carry):
            there, lo, device = ring_peer(q)
            remote(
                ring_out.at[s, pl.ds(lo * 4, 4), :, pl.ds(col, width)],
                ring_in.at[s, :, pl.ds(z * 16, 16), pl.ds(col, width)],
                fzs.at[k], fzr.at[k], device,
            ).start()
            return carry

        lax.fori_loop(1, RING, one, 0)
        ring_in[s, :, pl.ds(z * 16, 16), pl.ds(col, width)] = ring_out[
            s, pl.ds(z_lo * 4, 4), :, pl.ds(col, width)
        ]

    ring_send(1)
    ring_send(2)
    first_spread()
    for k in range(NF // 2, NF):
        ring_send(k)

    load_so.wait()
    for k, part_of in enumerate(split(so[...])):
        so_s[k] = dot_nn(to_order_t, part_of).astype(BF16)
    comb_grad = three(dot_nt, (og_s[0], og_s[1]), (so_s[0], so_s[1]))
    combine = comb[...]
    comb_term[...] = combine * (
        comb_grad - jnp.sum(comb_grad * combine, axis=1, keepdims=True)
    )

    load_wi.wait()
    load_wo.wait()

    def ring_arrived(k):
        s, col, width = FORWARD[k]
        wait_bytes(ring_in.at[s, :, pl.ds(0, 112), pl.ds(col, width)], fzr.at[k])
        across(k).start()

    def expert(k):
        s, col, width = FORWARD[k]
        across(k).wait_recv()

        def tile(t, carry):
            c = pl.multiple_of(t * 256, 256)
            first, second = None, None
            for h in range(2):
                d = h * HALF + col
                rows_in = ring_in[s, 2 * h, :, col : col + width]
                rows_grad = ring_in[s, 2 * h + 1, :, col : col + width]
                one = dot_nn(rows_in, wi[pl.ds(d, width), pl.ds(c, 256)])
                two = dot_nt(rows_grad, wo[pl.ds(c, 256), pl.ds(d, width)])
                first = one if first is None else first + one
                second = two if second is None else second + two
            if col > 0:
                first = first + acc[0, s, :, pl.ds(c, 256)]
                second = second + acc[1, s, :, pl.ds(c, 256)]
            if col + width == HALF:
                pre_grad[s, :, pl.ds(c, 256)] = (second * gelu_slope(first)).astype(BF16)
            else:
                acc[0, s, :, pl.ds(c, 256)] = first
                acc[1, s, :, pl.ds(c, 256)] = second
            return carry

        lax.fori_loop(0, 5, tile, 0)

    def back_across(s, b):
        col, width = BACK[b]
        return remote(
            part.at[s, :, pl.ds(128, 128), pl.ds(col, width)],
            part_in.at[s, :, :, pl.ds(col, width)],
            bcs.at[s, b], bcr.at[s, b], other,
        )

    def expert_back(s, b):
        col, width = BACK[b]
        for h in range(2):
            part[s, h, :, col : col + width] = dot_nt(
                pre_grad[s], wi[h * HALF + col : h * HALF + col + width, :]
            )
        back_across(s, b).start()

    def back_ring(s, b):
        col, width = BACK[b]
        back_across(s, b).wait_recv()
        both = part[s, :, 0:128, col : col + width] + part_in[s, :, :, col : col + width]
        back_out[s, :, :, col : col + width] = both.astype(BF16)

        def one(q, carry):
            there, _, device = ring_peer(q)
            remote(
                back_out.at[s, :, pl.ds(there * 16, 16), pl.ds(col, width)],
                back_in.at[s, :, pl.ds(z * 16, 16), pl.ds(col, width)],
                bzs.at[s, b], bzr.at[s, b], device,
            ).start()
            return carry

        lax.fori_loop(1, RING, one, 0)
        back_in[s, :, pl.ds(z * 16, 16), pl.ds(col, width)] = back_out[
            s, :, pl.ds(z * 16, 16), pl.ds(col, width)
        ]

    def back_plane(s, b):
        col, width = BACK[b]
        wait_bytes(back_in.at[s, :, pl.ds(0, 112), pl.ds(col, width)], bzr.at[s, b])
        back_send[s, :, col : col + width] = dot_nn(
            collect, back_in[s, :, :, col : col + width].reshape(ROWS, width)
        )

        def one(q, carry):
            there, device = plane_peer(q)
            remote(
                back_send.at[s, pl.ds(there * 8, 8), pl.ds(col, width)],
                sig.at[s, pl.ds(pos * 8, 8), pl.ds(col, width)],
                bps.at[s, b], bpr.at[s, b], device,
            ).start()
            return carry

        lax.fori_loop(1, PLANE, one, 0)
        sig[s, pl.ds(pos * 8, 8), pl.ds(col, width)] = back_send[
            s, pl.ds(pos * 8, 8), pl.ds(col, width)
        ]

    def arrived(s, b):
        col, width = BACK[b]
        wait_bytes(sig.at[s, pl.ds(0, 120), pl.ds(col, width)], bpr.at[s, b])
        high, low = split(sig[s, :, col : col + width])
        for h in range(2):
            c = h * HALF + col
            there = place(s, h)
            grad = (dot_nn(there, high).astype(BF16), dot_nn(there, low).astype(BF16))
            tokens = (acts_s[0, :, c : c + width], acts_s[1, :, c : c + width])
            term = three(dot_nt, tokens, grad)
            if s == 0 and b == 0 and h == 0:
                disp_grad[...] = term
            else:
                disp_grad[...] += term
            for k in range(2):
                grad_s[k, s * 64 : s * 64 + 64, c : c + width] = grad[k][s * 64 : s * 64 + 64]

    def proj_across(s):
        return remote(dp_out.at[s], dp_in.at[s], dps.at[s, 0], dpr.at[s, 0], other)

    def proj_start(s):
        dispatch = disp[...]
        grad = disp_grad[...]
        whole = comb_term[...] + dispatch * (
            grad - jnp.sum(grad * dispatch, axis=0, keepdims=True)
        )
        logit_grad[...] = whole
        rows = [dot_nn(twice(s), a).astype(BF16) for a in split(whole.T)]
        upper = lax.rem(lax.div(iota2((SLOTS, 384), 0), 4), 2) == 0

        def half(which):
            terms = []
            for k in range(2):
                cols = pl.ds(pl.multiple_of(k * HALF + which * 256, 128), 384)
                terms.append(three(dot_nn, rows, (acts_s[0, :, cols], acts_s[1, :, cols])))
            return jnp.where(upper, terms[0], terms[1])

        dp_out[s] = half(1 - core)
        proj_across(s).start()
        dp_own[s] = half(core)

    def proj_plane(s):
        proj_across(s).wait_recv()
        dp_sum[s] = dp_own[s] + dp_in[s]

        def one(q, carry):
            there, device = plane_peer(q)
            remote(
                dp_sum.at[s, pl.ds(there * 8, 8)], dp_plane.at[s, pl.ds(pos * 8, 8)],
                dps.at[s, 1], dpr.at[s, 1], device,
            ).start()
            return carry

        lax.fori_loop(1, PLANE, one, 0)
        dp_plane[s, pl.ds(pos * 8, 8)] = dp_sum[s, pl.ds(pos * 8, 8)]

    def proj_ring(s):
        wait_bytes(dp_plane.at[s, pl.ds(0, 120)], dpr.at[s, 1])
        dp_ring[s] = jnp.sum(dp_plane[s].reshape(PLANE, 8, 384), axis=0)

        def one(q, carry):
            there, _, device = ring_peer(q)
            remote(
                dp_ring.at[s], dp_back.at[s, pl.ds(z * 8, 8)],
                dps.at[s, 2], dpr.at[s, 2], device,
            ).start()
            return carry

        lax.fori_loop(1, RING, one, 0)
        dp_back[s, pl.ds(z * 8, 8)] = dp_ring[s]

    def proj_end(s):
        wait_bytes(dp_back.at[s, pl.ds(0, 56)], dpr.at[s, 2])
        total = jnp.sum(dp_back[s].reshape(RING, 8, 384), axis=0)
        mine = jnp.sum(
            jnp.where(iota2((8, 384), 0) == z, total, 0.0), axis=0, keepdims=True
        )
        dproj_ref[s : s + 1, :] = jnp.where(core == 0, mine[:, 0:320], mine[:, 64:384])

    first_arrived()
    for k in range(1, NF // 2 + 1):
        ring_arrived(k)
        expert(k - 1)
    for b in range(NB):
        expert_back(0, b)
    ring_arrived(4)
    for b in range(NB):
        back_ring(0, b)
    expert(3)
    ring_arrived(5)
    expert(4)
    expert(5)
    for b in range(NB):
        expert_back(1, b)
        if b > 0:
            back_ring(1, b - 1)
    back_ring(1, NB - 1)
    for b in range(NB):
        back_plane(0, b)
    back_plane(1, 0)
    arrived(0, 0)
    arrived(0, 1)
    back_plane(1, 1)
    arrived(0, 2)
    back_plane(1, 2)
    proj_start(0)
    arrived(1, 0)
    proj_plane(0)
    arrived(1, 1)
    arrived(1, 2)
    proj_start(1)
    proj_plane(1)
    proj_ring(0)
    whole = split(logit_grad[...])
    for c in range(0, D, 256):
        dacts[:, c : c + 256] = three(
            dot_nn, (disp_s[0], disp_s[1]), (grad_s[0, :, c : c + 256], grad_s[1, :, c : c + 256])
        ) + three(dot_nt, whole, (sp_s[0, c : c + 256, :], sp_s[1, c : c + 256, :]))
    proj_ring(1)
    proj_end(0)
    proj_end(1)

    for k in range(NF):
        s, col, width = FORWARD[k]
        if k == 0:
            wait_bytes(first_plane.at[:, pl.ds(0, 240)], fps.at[k])
            wait_bytes(first_in.at[:, pl.ds(0, 112)], fzs.at[k])
        else:
            wait_bytes(plane_in.at[s, pl.ds(0, 240), pl.ds(col, width)], fps.at[k])
            wait_bytes(ring_in.at[s, :, pl.ds(0, 112), pl.ds(col, width)], fzs.at[k])
        across(k).wait_send()
    for s in range(2):
        for b in range(NB):
            col, width = BACK[b]
            back_across(s, b).wait_send()
            wait_bytes(back_in.at[s, :, pl.ds(0, 112), pl.ds(col, width)], bzs.at[s, b])
            wait_bytes(sig.at[s, pl.ds(0, 120), pl.ds(col, width)], bps.at[s, b])
        proj_across(s).wait_send()
        wait_bytes(dp_plane.at[s, pl.ds(0, 120)], dps.at[s, 1])
        wait_bytes(dp_back.at[s, pl.ds(0, 56)], dps.at[s, 2])


def local(activations, out_grad, slot_out, slot_proj, w_in, w_out):
    vmem = pltpu.VMEM
    sems = pltpu.SemaphoreType.DMA
    any_space = pl.BlockSpec(memory_space=pl.ANY)
    d_acts, d_proj = pl.pallas_call(
        kernel,
        out_shape=(
            pltpu.VMEM((TOKENS, D), F32),
            pltpu.VMEM((2, 320), F32),
        ),
        in_specs=[any_space] * 6,
        out_specs=(pl.BlockSpec(memory_space=pltpu.VMEM),) * 2,
        scratch_shapes=[
            vmem((TOKENS, D), F32),
            vmem((TOKENS, D), F32),
            vmem((SLOTS, D), F32),
            vmem((D, SLOTS), F32),
            vmem((D, D), BF16),
            vmem((D, D), BF16),
            vmem((2, TOKENS, D), BF16),
            vmem((2, TOKENS, D), BF16),
            vmem((2, SLOTS, D), BF16),
            vmem((2, D, SLOTS), BF16),
            vmem((2, TOKENS, SLOTS), BF16),
            vmem((TOKENS, SLOTS), F32),
            vmem((TOKENS, SLOTS), F32),
            vmem((TOKENS, SLOTS), F32),
            vmem((TOKENS, SLOTS), F32),
            vmem((TOKENS, SLOTS), F32),
            vmem((2, SLOTS, D), BF16),
            vmem((2, SLOTS, D), BF16),
            vmem((2, ROWS, HALF), BF16),
            vmem((2, ROWS, HALF), BF16),
            vmem((2, 16, 16, HALF), BF16),
            vmem((2, 4, ROWS, HALF), BF16),
            vmem((16, 16, WIDE), BF16),
            vmem((4, 128, WIDE), BF16),
            vmem((2, ROWS, WIDE), BF16),
            vmem((2, ROWS, WIDE), BF16),
            vmem((2, 2, ROWS, D), F32),
            vmem((2, ROWS, D), BF16),
            vmem((2, 2, ROWS, HALF), F32),
            vmem((2, 2, 128, HALF), F32),
            vmem((2, 2, 128, HALF), BF16),
            vmem((2, 2, 128, HALF), BF16),
            vmem((2, SLOTS, HALF), F32),
            vmem((2, SLOTS, HALF), F32),
            vmem((2, SLOTS, 384), F32),
            vmem((2, SLOTS, 384), F32),
            vmem((2, SLOTS, 384), F32),
            vmem((2, SLOTS, 384), F32),
            vmem((2, SLOTS, 384), F32),
            vmem((2, 8, 384), F32),
            vmem((2, 64, 384), F32),
            sems((6,)),
            sems((NF,)), sems((NF,)), sems((NF,)), sems((NF,)), sems((NF,)), sems((NF,)),
            sems((2, NB)), sems((2, NB)), sems((2, NB)), sems((2, NB)), sems((2, NB)), sems((2, NB)),
            sems((2, 3)), sems((2, 3)),
        ],
        compiler_params=pltpu.CompilerParams(
            collective_id=0, has_side_effects=True, vmem_limit_bytes=56 * 2**20
        ),
        name="soft_moe_backward",
    )(activations[0], out_grad[0], slot_out[0], slot_proj, w_in[0], w_out[0])
    return d_acts[None], d_proj.T


def solution(mesh):
    placed = (
        P(("ep", "tp"), None, None),
        P(("ep", "tp"), None, None),
        P(("ep", "tp"), None, None),
        P(),
        P("ep", None, "tp"),
        P("ep", "tp", None),
    )
    return jax.shard_map(
        local,
        mesh=mesh,
        in_specs=placed,
        out_specs=(P(("ep", "tp"), None, None), P("tp", "ep")),
        check_vma=False,
    )
```

```python
import functools

import jax
import jax.numpy as jnp
from jax import lax
from jax.experimental import pallas as pl
from jax.experimental.pallas import tpu as pltpu
from jax.sharding import PartitionSpec as P

MESH = pl.DeviceIdType.MESH
F32 = jnp.float32
BF16 = jnp.bfloat16
D = 1280
HALF = 640
TOKENS = 256
SLOTS = 128
ROWS = 256
PLANE = 16
RING = 8
WIDE = 256
BLOCKS_A = ((0, 0), (0, 256), (0, 512), (0, 768))
BLOCKS_A1 = ((0, 0), (0, 128), (0, 256), (0, 384))
BLOCKS_A2 = ((0, 512), (0, 640), (0, 768), (0, 896))
BLOCKS_B = ((0, 1024), (1, 0), (1, 256), (1, 512))
BLOCKS_C = ((1, 768), (1, 896), (1, 1024), (1, 1152))
FORWARD = (
    (0, 0, 256, BLOCKS_A), (1, 0, 128, BLOCKS_A1),
    (0, 256, 256, BLOCKS_B), (0, 512, 128, BLOCKS_C),
    (1, 128, 128, BLOCKS_A2), (1, 256, 256, BLOCKS_B), (1, 512, 128, BLOCKS_C),
)
BACK = ((0, 128), (128, 256), (384, 128), (512, 128))
NF, NB = len(FORWARD), len(BACK)


def gelu_slope(pre_act):
    normal_cdf = 0.5 * (1.0 + lax.erf(pre_act * 0.7071067811865476))
    density = jnp.exp(-0.5 * pre_act * pre_act) * 0.3989422804014327
    return normal_cdf + pre_act * density


def dot_nn(a, b):
    return jnp.dot(a, b, preferred_element_type=F32)


def dot_nt(a, b):
    return lax.dot_general(a, b, (((1,), (1,)), ((), ())), preferred_element_type=F32)


def split(a):
    high = a.astype(BF16)
    return high, (a - high.astype(F32)).astype(BF16)


def three(dot, a, b):
    return dot(a[0], b[0]) + (dot(a[0], b[1]) + dot(a[1], b[0]))


def iota2(shape, axis):
    return lax.broadcasted_iota(jnp.int32, shape, axis)


def one_hot(condition):
    return jnp.where(condition, 1.0, 0.0).astype(BF16)


def kernel(
    acts_hbm, og_hbm, so_hbm, sp_hbm, wi_hbm, wo_hbm,
    dacts, dproj_ref,
    acts, og, so, sp, wi, wo,
    acts_s, og_s, so_s, sp_s, disp_s, disp, comb, comb_term, disp_grad, logit_grad, grad_s,
    slots, send, plane_in, ring_out, ring_in, first_out, first_in, first_send, first_plane,
    acc, pre_grad, part, part_in, back_out, back_in, back_send, sig,
    dp_out, dp_own, dp_in, dp_sum, dp_plane, dp_pack, dp_back,
    load_sem, fps, fpr, fzs, fzr, fcs, fcr, bcs, bcr, bzs, bzr, bps, bpr, dps, dpr,
):
    ep, tp = lax.axis_index("ep"), lax.axis_index("tp")
    z_lo, pos = lax.div(ep, 16), lax.rem(ep, 16)
    x, y = lax.div(pos, 4), lax.rem(pos, 4)
    z_hi, core = lax.div(tp, 2), lax.rem(tp, 2)
    z = z_hi * 4 + z_lo
    other = {"ep": ep, "tp": z_hi * 2 + (1 - core)}

    def plane_peer(i):
        q = 1 + lax.rem(i + 8, PLANE - 1)
        there = lax.rem(x + lax.div(q, 4), 4) * 4 + lax.rem(y + lax.rem(q, 4), 4)
        return there, {"ep": z_lo * 16 + there, "tp": tp}

    def ring_peer(i):
        q = 1 + lax.rem(i + 2, RING - 1)
        there = lax.rem(z + q, RING)
        lo = lax.rem(there, 4)
        return there, lo, {"ep": lo * 16 + pos, "tp": lax.div(there, 4) * 2 + core}

    def remote(src, dst, send_sem, recv_sem, device):
        return pltpu.make_async_remote_copy(
            src_ref=src, dst_ref=dst, send_sem=send_sem, recv_sem=recv_sem,
            device_id=device, device_id_type=MESH,
        )

    def wait_bytes(ref, sem):
        pltpu.make_async_copy(ref, ref, sem).wait()

    loads = []
    pairs = ((sp_hbm, sp), (acts_hbm, acts), (og_hbm, og), (so_hbm, so), (wi_hbm, wi), (wo_hbm, wo))
    for k, (src, dst) in enumerate(pairs):
        loads.append(pltpu.make_async_copy(src, dst, load_sem.at[k]))
        if k < 3:
            loads[-1].start()
    load_sp, load_acts, load_og, load_so, load_wi, load_wo = loads

    barrier = pltpu.get_barrier_semaphore()

    def greet_plane(q, carry):
        pl.semaphore_signal(barrier, inc=1, device_id=plane_peer(q)[1], device_id_type=MESH)
        return carry

    def greet_ring(q, carry):
        pl.semaphore_signal(barrier, inc=1, device_id=ring_peer(q)[2], device_id_type=MESH)
        return carry

    lax.fori_loop(0, PLANE - 1, greet_plane, 0)
    lax.fori_loop(0, RING - 1, greet_ring, 0)
    pl.semaphore_signal(barrier, inc=1, device_id=other, device_id_type=MESH)

    n, r = iota2((SLOTS, SLOTS), 0), iota2((SLOTS, SLOTS), 1)
    to_order = one_hot(n == lax.rem(r, 4) * 32 + lax.rem(lax.div(r, 4), 16) * 2 + lax.div(r, 64))
    to_order_t = one_hot(r == lax.rem(n, 4) * 32 + lax.rem(lax.div(n, 4), 16) * 2 + lax.div(n, 64))
    o, i = iota2((ROWS, ROWS), 0), iota2((ROWS, ROWS), 1)
    spread = one_hot(
        i == lax.rem(lax.div(o, 4), 4) * 64 + lax.div(o, 16) * 4 + lax.rem(o, 4)
    )
    regroup = one_hot(
        i == lax.rem(o, 16) * 16 + lax.rem(lax.div(o, 16), 4) * 4 + lax.div(o, 64)
    )
    direct = one_hot(
        i == lax.rem(lax.div(o, 16), 4) * 64 + lax.rem(o, 16) * 4 + lax.div(o, 64)
    )
    to_plane = one_hot(
        i == lax.rem(lax.div(o, 8), 2) * 128 + lax.rem(o, 8) * 16 + lax.div(o, 16)
    )
    from_plane = one_hot(
        o == lax.rem(lax.div(i, 8), 2) * 128 + lax.rem(i, 8) * 16 + lax.div(i, 16)
    )
    o, i = iota2((SLOTS, ROWS), 0), iota2((SLOTS, ROWS), 1)
    collect = one_hot(
        (lax.div(i, 128) == lax.rem(lax.div(o, 4), 2))
        & (lax.rem(i, 64) == lax.rem(o, 4) * 16 + lax.div(o, 8))
    )
    def place(s, h):
        return one_hot(
            (lax.div(n, 64) == s)
            & (r == lax.div(lax.rem(n, 64), 4) * 8 + h * 4 + lax.rem(n, 4))
        )

    def twice(s):
        return one_hot(r == s * 64 + lax.div(n, 8) * 4 + lax.rem(n, 4))

    dp_pack[...] = jnp.zeros_like(dp_pack)
    load_sp.wait()
    for k, part_of in enumerate(split(sp[...])):
        sp_s[k] = dot_nn(part_of, to_order).astype(BF16)
    load_acts.wait()
    for late in (load_so, load_wi, load_wo):
        late.start()
    acts_s[0], acts_s[1] = split(acts[...])
    logits = three(dot_nn, (acts_s[0], acts_s[1]), (sp_s[0], sp_s[1]))
    e = jnp.exp(logits - jnp.max(logits, axis=0, keepdims=True))
    dispatch = e / jnp.sum(e, axis=0, keepdims=True)
    disp[...] = dispatch
    disp_s[0], disp_s[1] = split(dispatch)
    dispatch_t = split(dispatch.T)

    def slot_rows(kind, weights_t, values, c):
        rows = three(dot_nn, weights_t, (values[0, :, c : c + WIDE], values[1, :, c : c + WIDE]))
        slots[kind, :, c : c + WIDE] = rows.astype(BF16)

    def across(k):
        s, col, width, blocks = FORWARD[k]
        return remote(
            ring_in.at[s, :, pl.ds(0, 128), pl.ds(col, width)],
            ring_in.at[s, :, pl.ds(128, 128), pl.ds(col, width)],
            fcs.at[k], fcr.at[k], other,
        )

    def stacked(k):
        s, col, width, blocks = FORWARD[k]
        parts = [
            slots[kind, s * 64 : s * 64 + 64, c : c + width] for kind, c in blocks
        ]
        return jnp.concatenate(parts, axis=0)

    def first_ring(k):
        width = FORWARD[k][2]
        rows = dot_nn(direct, stacked(k)).astype(BF16)
        first_out[k, :, :, 0:width] = rows.reshape(16, 16, width)
        if k == 0:
            pl.semaphore_wait(barrier, PLANE - 1 + RING - 1 + 1)

        def one(q, carry):
            there, lo, device = ring_peer(q)
            remote(
                first_out.at[k, pl.ds(lo * 4, 4), :, pl.ds(0, width)],
                first_in.at[k, :, pl.ds(z * 16, 16), pl.ds(0, width)],
                fzs.at[k], fzr.at[k], device,
            ).start()
            return carry

        lax.fori_loop(0, RING - 1, one, 0)
        first_in[k, :, pl.ds(z * 16, 16), 0:width] = first_out[k, pl.ds(z_lo * 4, 4), :, 0:width]

    def first_spread(k):
        width = FORWARD[k][2]
        wait_bytes(first_in.at[k, :, pl.ds(0, 112), pl.ds(0, width)], fzr.at[k])
        for h in range(2):
            rows = first_in[k, 2 * h : 2 * h + 2, :, 0:width].reshape(ROWS, width)
            first_send[k, h, :, 0:width] = dot_nn(to_plane, rows).astype(BF16)

        def one(q, carry):
            there, device = plane_peer(q)
            remote(
                first_send.at[k, :, pl.ds(there * 16, 16), pl.ds(0, width)],
                first_plane.at[k, :, pl.ds(pos * 16, 16), pl.ds(0, width)],
                fps.at[k], fpr.at[k], device,
            ).start()
            return carry

        lax.fori_loop(0, PLANE - 1, one, 0)
        first_plane[k, :, pl.ds(pos * 16, 16), 0:width] = first_send[
            k, :, pl.ds(pos * 16, 16), 0:width
        ]

    def first_arrived(k):
        s, col, width, blocks = FORWARD[k]
        wait_bytes(first_plane.at[k, :, pl.ds(0, 240), pl.ds(0, width)], fpr.at[k])
        for h in range(2):
            rows = dot_nn(from_plane, first_plane[k, h, :, 0:width]).astype(BF16)
            ring_in[s, 2 * h : 2 * h + 2, 0:128, col : col + width] = rows.reshape(2, 128, width)
        across(k).start()

    def plane_send(k):
        s, col, width, blocks = FORWARD[k]
        send[s, :, col : col + width] = dot_nn(spread, stacked(k)).astype(BF16)

        def one(q, carry):
            there, device = plane_peer(q)
            remote(
                send.at[s, pl.ds(there * 16, 16), pl.ds(col, width)],
                plane_in.at[s, pl.ds(pos * 16, 16), pl.ds(col, width)],
                fps.at[k], fpr.at[k], device,
            ).start()
            return carry

        lax.fori_loop(0, PLANE - 1, one, 0)
        plane_in[s, pl.ds(pos * 16, 16), pl.ds(col, width)] = send[
            s, pl.ds(pos * 16, 16), pl.ds(col, width)
        ]

    for c in range(0, D - WIDE, WIDE):
        slot_rows(0, dispatch_t, acts_s, c)
    first_ring(0)
    first_ring(1)
    slot_rows(0, dispatch_t, acts_s, D - WIDE)
    e = jnp.exp(logits - jnp.max(logits, axis=1, keepdims=True))
    combine = e / jnp.sum(e, axis=1, keepdims=True)
    comb[...] = combine
    combine_t = split(combine.T)
    load_og.wait()
    for c in range(0, D, WIDE):
        og_s[0, :, c : c + WIDE], og_s[1, :, c : c + WIDE] = split(og[:, c : c + WIDE])
        slot_rows(1, combine_t, og_s, c)
        if c == 512:
            plane_send(2)
    for k in range(3, NF):
        plane_send(k)

    def ring_send(k):
        s, col, width, blocks = FORWARD[k]
        wait_bytes(plane_in.at[s, pl.ds(0, 240), pl.ds(col, width)], fpr.at[k])
        moved = dot_nn(regroup, plane_in[s, :, col : col + width])
        ring_out[s, :, :, col : col + width] = moved.astype(BF16).reshape(16, 16, width)

        def one(q, carry):
            there, lo, device = ring_peer(q)
            remote(
                ring_out.at[s, pl.ds(lo * 4, 4), :, pl.ds(col, width)],
                ring_in.at[s, :, pl.ds(z * 16, 16), pl.ds(col, width)],
                fzs.at[k], fzr.at[k], device,
            ).start()
            return carry

        lax.fori_loop(0, RING - 1, one, 0)
        ring_in[s, :, pl.ds(z * 16, 16), pl.ds(col, width)] = ring_out[
            s, pl.ds(z_lo * 4, 4), :, pl.ds(col, width)
        ]

    ring_send(2)
    first_spread(0)
    for k in range(3, NF):
        ring_send(k)

    load_so.wait()
    for k, part_of in enumerate(split(so[...])):
        so_s[k] = dot_nn(to_order_t, part_of).astype(BF16)
    comb_grad = three(dot_nt, (og_s[0], og_s[1]), (so_s[0], so_s[1]))
    combine = comb[...]
    comb_term[...] = combine * (
        comb_grad - jnp.sum(comb_grad * combine, axis=1, keepdims=True)
    )

    load_wi.wait()
    load_wo.wait()

    def ring_arrived(k):
        s, col, width, blocks = FORWARD[k]
        wait_bytes(ring_in.at[s, :, pl.ds(0, 112), pl.ds(col, width)], fzr.at[k])
        across(k).start()

    def expert(k):
        s, col, width, blocks = FORWARD[k]
        across(k).wait_recv()

        def tile(t, carry):
            c = pl.multiple_of(t * 256, 256)
            sums = [None, None]
            step = WIDE // width
            for j in range(0, 4, step):
                kind, d = blocks[j]
                rows = [ring_in[s, j + i, :, col : col + width] for i in range(step)]
                rows = rows[0] if step == 1 else jnp.concatenate(rows, axis=1)
                if kind == 0:
                    term = dot_nn(rows, wi[pl.ds(d, WIDE), pl.ds(c, 256)])
                else:
                    term = dot_nt(rows, wo[pl.ds(c, 256), pl.ds(d, WIDE)])
                sums[kind] = term if sums[kind] is None else sums[kind] + term
            here = pl.ds(c, 256)
            if blocks is BLOCKS_A or blocks is BLOCKS_A1:
                acc[0, s, :, here] = sums[0]
            elif blocks is BLOCKS_A2:
                acc[0, s, :, here] += sums[0]
            elif blocks is BLOCKS_B:
                acc[0, s, :, here] = gelu_slope(acc[0, s, :, here] + sums[0])
                acc[1, s, :, here] = sums[1]
            else:
                hidden_grad = acc[1, s, :, here] + sums[1]
                pre_grad[s, :, here] = (hidden_grad * acc[0, s, :, here]).astype(BF16)
            return carry

        lax.fori_loop(0, 5, tile, 0)

    def back_across(s, b):
        col, width = BACK[b]
        return remote(
            part.at[s, :, pl.ds(128, 128), pl.ds(col, width)],
            part_in.at[s, :, :, pl.ds(col, width)],
            bcs.at[s, b], bcr.at[s, b], other,
        )

    def expert_back(s, b):
        col, width = BACK[b]
        for h in range(2):
            part[s, h, :, col : col + width] = dot_nt(
                pre_grad[s], wi[h * HALF + col : h * HALF + col + width, :]
            )
        back_across(s, b).start()

    def back_ring(s, b):
        col, width = BACK[b]
        back_across(s, b).wait_recv()
        both = part[s, :, 0:128, col : col + width] + part_in[s, :, :, col : col + width]
        back_out[s, :, :, col : col + width] = both.astype(BF16)

        def one(q, carry):
            there, _, device = ring_peer(q)
            remote(
                back_out.at[s, :, pl.ds(there * 16, 16), pl.ds(col, width)],
                back_in.at[s, :, pl.ds(z * 16, 16), pl.ds(col, width)],
                bzs.at[s, b], bzr.at[s, b], device,
            ).start()
            return carry

        lax.fori_loop(0, RING - 1, one, 0)
        back_in[s, :, pl.ds(z * 16, 16), pl.ds(col, width)] = back_out[
            s, :, pl.ds(z * 16, 16), pl.ds(col, width)
        ]

    def back_plane(s, b):
        col, width = BACK[b]
        wait_bytes(back_in.at[s, :, pl.ds(0, 112), pl.ds(col, width)], bzr.at[s, b])
        back_send[s, :, col : col + width] = dot_nn(
            collect, back_in[s, :, :, col : col + width].reshape(ROWS, width)
        )

        def one(q, carry):
            there, device = plane_peer(q)
            remote(
                back_send.at[s, pl.ds(there * 8, 8), pl.ds(col, width)],
                sig.at[s, pl.ds(pos * 8, 8), pl.ds(col, width)],
                bps.at[s, b], bpr.at[s, b], device,
            ).start()
            return carry

        lax.fori_loop(0, PLANE - 1, one, 0)
        sig[s, pl.ds(pos * 8, 8), pl.ds(col, width)] = back_send[
            s, pl.ds(pos * 8, 8), pl.ds(col, width)
        ]

    def arrived(s, b):
        col, width = BACK[b]
        wait_bytes(sig.at[s, pl.ds(0, 120), pl.ds(col, width)], bpr.at[s, b])
        high, low = split(sig[s, :, col : col + width])
        for h in range(2):
            c = h * HALF + col
            there = place(s, h)
            grad = (dot_nn(there, high).astype(BF16), dot_nn(there, low).astype(BF16))
            tokens = (acts_s[0, :, c : c + width], acts_s[1, :, c : c + width])
            term = three(dot_nt, tokens, grad)
            if s == 0 and b == 0 and h == 0:
                disp_grad[...] = term
            else:
                disp_grad[...] += term
            for k in range(2):
                grad_s[k, s * 64 : s * 64 + 64, c : c + width] = grad[k][s * 64 : s * 64 + 64]

    def proj_across(s):
        return remote(dp_out.at[s], dp_in.at[s], dps.at[s, 0], dpr.at[s, 0], other)

    def proj_start(s):
        dispatch = disp[...]
        grad = disp_grad[...]
        whole = comb_term[...] + dispatch * (
            grad - jnp.sum(grad * dispatch, axis=0, keepdims=True)
        )
        logit_grad[...] = whole
        rows = [dot_nn(twice(s), a).astype(BF16) for a in split(whole.T)]
        upper = lax.rem(lax.div(iota2((SLOTS, 384), 0), 4), 2) == 0

        def half(which):
            terms = []
            for k in range(2):
                cols = pl.ds(pl.multiple_of(k * HALF + which * 256, 128), 384)
                terms.append(three(dot_nn, rows, (acts_s[0, :, cols], acts_s[1, :, cols])))
            return jnp.where(upper, terms[0], terms[1])

        dp_out[s] = half(1 - core)
        proj_across(s).start()
        dp_own[s] = half(core)

    def proj_plane(s):
        proj_across(s).wait_recv()
        dp_sum[s] = dp_own[s] + dp_in[s]

        def one(q, carry):
            there, device = plane_peer(q)
            remote(
                dp_sum.at[s, pl.ds(there * 8, 8)], dp_plane.at[s, pl.ds(pos * 8, 8)],
                dps.at[s, 1], dpr.at[s, 1], device,
            ).start()
            return carry

        lax.fori_loop(0, PLANE - 1, one, 0)
        dp_plane[s, pl.ds(pos * 8, 8)] = dp_sum[s, pl.ds(pos * 8, 8)]

    def proj_pack(s):
        wait_bytes(dp_plane.at[s, pl.ds(0, 120)], dpr.at[s, 1])
        total = jnp.sum(dp_plane[s].reshape(PLANE, 8, 384), axis=0)
        for k in range(3):
            dp_pack[:, s * 3 + k, :] = total[:, k * 128 : k * 128 + 128]

    def proj_ring():
        def one(q, carry):
            there, _, device = ring_peer(q)
            remote(
                dp_pack.at[there], dp_back.at[z], dps.at[0, 2], dpr.at[0, 2], device
            ).start()
            return carry

        lax.fori_loop(0, RING - 1, one, 0)
        dp_back[z] = dp_pack[z]

    def proj_end():
        wait_bytes(dp_back.at[pl.ds(0, 7)], dpr.at[0, 2])
        total = jnp.sum(dp_back[...], axis=0)
        for s in range(2):
            mine = jnp.concatenate([total[s * 3 + k : s * 3 + k + 1] for k in range(3)], axis=1)
            dproj_ref[s : s + 1, :] = jnp.where(core == 0, mine[:, 0:320], mine[:, 64:384])

    first_spread(1)
    first_arrived(0)
    expert(0)
    ring_arrived(2)
    first_arrived(1)
    expert(2)
    ring_arrived(3)
    expert(1)
    expert(3)
    for b in range(NB):
        expert_back(0, b)
    ring_arrived(4)
    for b in range(NB):
        back_ring(0, b)
    expert(4)
    ring_arrived(5)
    expert(5)
    ring_arrived(6)
    expert(6)
    for b in range(NB):
        expert_back(1, b)
        if b > 0:
            back_ring(1, b - 1)
    back_ring(1, NB - 1)
    for b in range(NB):
        back_plane(0, b)
    back_plane(1, 0)
    arrived(0, 0)
    arrived(0, 1)
    back_plane(1, 1)
    arrived(0, 2)
    arrived(0, 3)
    back_plane(1, 2)
    back_plane(1, 3)
    proj_start(0)
    arrived(1, 0)
    proj_plane(0)
    arrived(1, 1)
    arrived(1, 2)
    arrived(1, 3)
    proj_start(1)
    proj_plane(1)
    proj_pack(0)
    whole = split(logit_grad[...])
    for c in range(0, D, 256):
        dacts[:, c : c + 256] = three(
            dot_nn, (disp_s[0], disp_s[1]), (grad_s[0, :, c : c + 256], grad_s[1, :, c : c + 256])
        ) + three(dot_nt, whole, (sp_s[0, c : c + 256, :], sp_s[1, c : c + 256, :]))
    proj_pack(1)
    proj_ring()
    proj_end()

    for k in range(NF):
        s, col, width, blocks = FORWARD[k]
        if k < 2:
            wait_bytes(first_plane.at[k, :, pl.ds(0, 240), pl.ds(0, width)], fps.at[k])
            wait_bytes(first_in.at[k, :, pl.ds(0, 112), pl.ds(0, width)], fzs.at[k])
        else:
            wait_bytes(plane_in.at[s, pl.ds(0, 240), pl.ds(col, width)], fps.at[k])
            wait_bytes(ring_in.at[s, :, pl.ds(0, 112), pl.ds(col, width)], fzs.at[k])
        across(k).wait_send()
    for s in range(2):
        for b in range(NB):
            col, width = BACK[b]
            back_across(s, b).wait_send()
            wait_bytes(back_in.at[s, :, pl.ds(0, 112), pl.ds(col, width)], bzs.at[s, b])
            wait_bytes(sig.at[s, pl.ds(0, 120), pl.ds(col, width)], bps.at[s, b])
        proj_across(s).wait_send()
        wait_bytes(dp_plane.at[s, pl.ds(0, 120)], dps.at[s, 1])
    wait_bytes(dp_back.at[pl.ds(0, 7)], dps.at[0, 2])


def local(activations, out_grad, slot_out, slot_proj, w_in, w_out):
    vmem = pltpu.VMEM
    sems = pltpu.SemaphoreType.DMA
    any_space = pl.BlockSpec(memory_space=pl.ANY)
    d_acts, d_proj = pl.pallas_call(
        kernel,
        out_shape=(
            pltpu.VMEM((TOKENS, D), F32),
            pltpu.VMEM((2, 320), F32),
        ),
        in_specs=[any_space] * 6,
        out_specs=(pl.BlockSpec(memory_space=pltpu.VMEM),) * 2,
        scratch_shapes=[
            vmem((TOKENS, D), F32),
            vmem((TOKENS, D), F32),
            vmem((SLOTS, D), F32),
            vmem((D, SLOTS), F32),
            vmem((D, D), BF16),
            vmem((D, D), BF16),
            vmem((2, TOKENS, D), BF16),
            vmem((2, TOKENS, D), BF16),
            vmem((2, SLOTS, D), BF16),
            vmem((2, D, SLOTS), BF16),
            vmem((2, TOKENS, SLOTS), BF16),
            vmem((TOKENS, SLOTS), F32),
            vmem((TOKENS, SLOTS), F32),
            vmem((TOKENS, SLOTS), F32),
            vmem((TOKENS, SLOTS), F32),
            vmem((TOKENS, SLOTS), F32),
            vmem((2, SLOTS, D), BF16),
            vmem((2, SLOTS, D), BF16),
            vmem((2, ROWS, HALF), BF16),
            vmem((2, ROWS, HALF), BF16),
            vmem((2, 16, 16, HALF), BF16),
            vmem((2, 4, ROWS, HALF), BF16),
            vmem((2, 16, 16, WIDE), BF16),
            vmem((2, 4, 128, WIDE), BF16),
            vmem((2, 2, ROWS, WIDE), BF16),
            vmem((2, 2, ROWS, WIDE), BF16),
            vmem((2, 2, ROWS, D), F32),
            vmem((2, ROWS, D), BF16),
            vmem((2, 2, ROWS, HALF), F32),
            vmem((2, 2, 128, HALF), F32),
            vmem((2, 2, 128, HALF), BF16),
            vmem((2, 2, 128, HALF), BF16),
            vmem((2, SLOTS, HALF), F32),
            vmem((2, SLOTS, HALF), F32),
            vmem((2, SLOTS, 384), F32),
            vmem((2, SLOTS, 384), F32),
            vmem((2, SLOTS, 384), F32),
            vmem((2, SLOTS, 384), F32),
            vmem((2, SLOTS, 384), F32),
            vmem((8, 8, 128), F32),
            vmem((8, 8, 128), F32),
            sems((6,)),
            sems((NF,)), sems((NF,)), sems((NF,)), sems((NF,)), sems((NF,)), sems((NF,)),
            sems((2, NB)), sems((2, NB)), sems((2, NB)), sems((2, NB)), sems((2, NB)), sems((2, NB)),
            sems((2, 3)), sems((2, 3)),
        ],
        compiler_params=pltpu.CompilerParams(
            collective_id=0, has_side_effects=True, vmem_limit_bytes=56 * 2**20
        ),
        name="soft_moe_backward",
    )(activations[0], out_grad[0], slot_out[0], slot_proj, w_in[0], w_out[0])
    return d_acts[None], d_proj.T


def solution(mesh):
    placed = (
        P(("ep", "tp"), None, None),
        P(("ep", "tp"), None, None),
        P(("ep", "tp"), None, None),
        P(),
        P("ep", None, "tp"),
        P("ep", "tp", None),
    )
    return jax.shard_map(
        local,
        mesh=mesh,
        in_specs=placed,
        out_specs=(P(("ep", "tp"), None, None), P("tp", "ep")),
        check_vma=False,
    )
```

```python
import functools

import jax
import jax.numpy as jnp
from jax import lax
from jax.experimental import pallas as pl
from jax.experimental.pallas import tpu as pltpu
from jax.sharding import PartitionSpec as P

MESH = pl.DeviceIdType.MESH
F32 = jnp.float32
BF16 = jnp.bfloat16
D = 1280
HALF = 640
TOKENS = 256
SLOTS = 128
ROWS = 256
PLANE = 16
RING = 8
WIDE = 256
BLOCKS_A = ((0, 0), (0, 256), (0, 512), (0, 768))
BLOCKS_A1 = ((0, 0), (0, 128), (0, 256), (0, 384))
BLOCKS_A2 = ((0, 512), (0, 640), (0, 768), (0, 896))
BLOCKS_B = ((0, 1024), (1, 0), (1, 256), (1, 512))
BLOCKS_C = ((1, 768), (1, 896), (1, 1024), (1, 1152))
FORWARD = (
    (0, 0, 256, BLOCKS_A), (1, 0, 128, BLOCKS_A1),
    (0, 256, 256, BLOCKS_B), (0, 512, 128, BLOCKS_C),
    (1, 128, 128, BLOCKS_A2), (1, 256, 256, BLOCKS_B), (1, 512, 128, BLOCKS_C),
)
BACK = ((0, 128), (128, 256), (384, 128), (512, 128))
NF, NB = len(FORWARD), len(BACK)


def gelu_slope(pre_act):
    normal_cdf = 0.5 * (1.0 + lax.erf(pre_act * 0.7071067811865476))
    density = jnp.exp(-0.5 * pre_act * pre_act) * 0.3989422804014327
    return normal_cdf + pre_act * density


def dot_nn(a, b):
    return jnp.dot(a, b, preferred_element_type=F32)


def dot_nt(a, b):
    return lax.dot_general(a, b, (((1,), (1,)), ((), ())), preferred_element_type=F32)


def split(a):
    high = a.astype(BF16)
    return high, (a - high.astype(F32)).astype(BF16)


def three(dot, a, b):
    return dot(a[0], b[0]) + (dot(a[0], b[1]) + dot(a[1], b[0]))


def iota2(shape, axis):
    return lax.broadcasted_iota(jnp.int32, shape, axis)


def one_hot(condition):
    return jnp.where(condition, 1.0, 0.0).astype(BF16)


def kernel(
    acts_hbm, og_hbm, so_hbm, sp_hbm, wi_hbm, wo_hbm,
    dacts, dproj_ref,
    acts, og, so, sp, wi, wo,
    acts_s, og_s, so_s, sp_s, disp_s, disp, comb, comb_term, disp_grad, logit_grad, grad_s,
    slots, send, plane_in, ring_out, ring_in, first_out, first_in, first_send, first_plane,
    acc, pre_grad, part, part_in, back_out, back_in, back_send, sig,
    dp_out, dp_own, dp_in, dp_sum, dp_plane, dp_pack, dp_back,
    load_sem, fps, fpr, fzs, fzr, fcs, fcr, bcs, bcr, bzs, bzr, bps, bpr, dps, dpr,
):
    ep, tp = lax.axis_index("ep"), lax.axis_index("tp")
    z_lo, pos = lax.div(ep, 16), lax.rem(ep, 16)
    x, y = lax.div(pos, 4), lax.rem(pos, 4)
    z_hi, core = lax.div(tp, 2), lax.rem(tp, 2)
    z = z_hi * 4 + z_lo
    other = {"ep": ep, "tp": z_hi * 2 + (1 - core)}

    def plane_peer(i):
        q = 1 + lax.rem(i + 8, PLANE - 1)
        there = lax.rem(x + lax.div(q, 4), 4) * 4 + lax.rem(y + lax.rem(q, 4), 4)
        return there, {"ep": z_lo * 16 + there, "tp": tp}

    def ring_peer(i):
        q = 1 + lax.rem(i + 2, RING - 1)
        there = lax.rem(z + q, RING)
        lo = lax.rem(there, 4)
        return there, lo, {"ep": lo * 16 + pos, "tp": lax.div(there, 4) * 2 + core}

    def remote(src, dst, send_sem, recv_sem, device):
        return pltpu.make_async_remote_copy(
            src_ref=src, dst_ref=dst, send_sem=send_sem, recv_sem=recv_sem,
            device_id=device, device_id_type=MESH,
        )

    def wait_bytes(ref, sem):
        pltpu.make_async_copy(ref, ref, sem).wait()

    loads = []
    pairs = ((sp_hbm, sp), (acts_hbm, acts), (og_hbm, og), (so_hbm, so), (wi_hbm, wi), (wo_hbm, wo))
    for k, (src, dst) in enumerate(pairs):
        loads.append(pltpu.make_async_copy(src, dst, load_sem.at[k]))
        if k < 3:
            loads[-1].start()
    load_sp, load_acts, load_og, load_so, load_wi, load_wo = loads

    barrier = pltpu.get_barrier_semaphore()

    def greet_plane(q, carry):
        pl.semaphore_signal(barrier, inc=1, device_id=plane_peer(q)[1], device_id_type=MESH)
        return carry

    def greet_ring(q, carry):
        pl.semaphore_signal(barrier, inc=1, device_id=ring_peer(q)[2], device_id_type=MESH)
        return carry

    lax.fori_loop(0, PLANE - 1, greet_plane, 0)
    lax.fori_loop(0, RING - 1, greet_ring, 0)
    pl.semaphore_signal(barrier, inc=1, device_id=other, device_id_type=MESH)

    n, r = iota2((SLOTS, SLOTS), 0), iota2((SLOTS, SLOTS), 1)
    to_order = one_hot(n == lax.rem(r, 4) * 32 + lax.rem(lax.div(r, 4), 16) * 2 + lax.div(r, 64))
    to_order_t = one_hot(r == lax.rem(n, 4) * 32 + lax.rem(lax.div(n, 4), 16) * 2 + lax.div(n, 64))
    o, i = iota2((ROWS, ROWS), 0), iota2((ROWS, ROWS), 1)
    spread = one_hot(
        i == lax.rem(lax.div(o, 4), 4) * 64 + lax.div(o, 16) * 4 + lax.rem(o, 4)
    )
    regroup = one_hot(
        i == lax.rem(o, 16) * 16 + lax.rem(lax.div(o, 16), 4) * 4 + lax.div(o, 64)
    )
    direct = one_hot(
        i == lax.rem(lax.div(o, 16), 4) * 64 + lax.rem(o, 16) * 4 + lax.div(o, 64)
    )
    to_plane = one_hot(
        i == lax.rem(lax.div(o, 8), 2) * 128 + lax.rem(o, 8) * 16 + lax.div(o, 16)
    )
    from_plane = one_hot(
        o == lax.rem(lax.div(i, 8), 2) * 128 + lax.rem(i, 8) * 16 + lax.div(i, 16)
    )
    o, i = iota2((SLOTS, ROWS), 0), iota2((SLOTS, ROWS), 1)
    collect = one_hot(
        (lax.div(i, 128) == lax.rem(lax.div(o, 4), 2))
        & (lax.rem(i, 64) == lax.rem(o, 4) * 16 + lax.div(o, 8))
    )
    def place(s, h):
        return one_hot(
            (lax.div(n, 64) == s)
            & (r == lax.div(lax.rem(n, 64), 4) * 8 + h * 4 + lax.rem(n, 4))
        )

    def twice(s):
        return one_hot(r == s * 64 + lax.div(n, 8) * 4 + lax.rem(n, 4))

    dp_pack[...] = jnp.zeros_like(dp_pack)
    load_sp.wait()
    for k, part_of in enumerate(split(sp[...])):
        sp_s[k] = dot_nn(part_of, to_order).astype(BF16)
    load_acts.wait()
    for late in (load_so, load_wi, load_wo):
        late.start()
    acts_s[0], acts_s[1] = split(acts[...])
    logits = three(dot_nn, (acts_s[0], acts_s[1]), (sp_s[0], sp_s[1]))
    e = jnp.exp(logits - jnp.max(logits, axis=0, keepdims=True))
    dispatch = e / jnp.sum(e, axis=0, keepdims=True)
    disp[...] = dispatch
    disp_s[0], disp_s[1] = split(dispatch)
    dispatch_t = split(dispatch.T)

    def slot_rows(kind, weights_t, values, c):
        rows = three(dot_nn, weights_t, (values[0, :, c : c + WIDE], values[1, :, c : c + WIDE]))
        slots[kind, :, c : c + WIDE] = rows.astype(BF16)

    def across(k):
        s, col, width, blocks = FORWARD[k]
        return remote(
            ring_in.at[s, :, pl.ds(0, 128), pl.ds(col, width)],
            ring_in.at[s, :, pl.ds(128, 128), pl.ds(col, width)],
            fcs.at[k], fcr.at[k], other,
        )

    def stacked(k):
        s, col, width, blocks = FORWARD[k]
        parts = [
            slots[kind, s * 64 : s * 64 + 64, c : c + width] for kind, c in blocks
        ]
        return jnp.concatenate(parts, axis=0)

    def first_ring(k):
        width = FORWARD[k][2]
        rows = dot_nn(direct, stacked(k)).astype(BF16)
        first_out[k, :, :, 0:width] = rows.reshape(16, 16, width)
        if k == 0:
            pl.semaphore_wait(barrier, PLANE - 1 + RING - 1 + 1)

        def one(q, carry):
            there, lo, device = ring_peer(q)
            remote(
                first_out.at[k, pl.ds(lo * 4, 4), :, pl.ds(0, width)],
                first_in.at[k, :, pl.ds(z * 16, 16), pl.ds(0, width)],
                fzs.at[k], fzr.at[k], device,
            ).start()
            return carry

        lax.fori_loop(0, RING - 1, one, 0)
        first_in[k, :, pl.ds(z * 16, 16), 0:width] = first_out[k, pl.ds(z_lo * 4, 4), :, 0:width]

    def first_spread(k):
        width = FORWARD[k][2]
        wait_bytes(first_in.at[k, :, pl.ds(0, 112), pl.ds(0, width)], fzr.at[k])
        for h in range(2):
            rows = first_in[k, 2 * h : 2 * h + 2, :, 0:width].reshape(ROWS, width)
            first_send[k, h, :, 0:width] = dot_nn(to_plane, rows).astype(BF16)

        def one(q, carry):
            there, device = plane_peer(q)
            remote(
                first_send.at[k, :, pl.ds(there * 16, 16), pl.ds(0, width)],
                first_plane.at[k, :, pl.ds(pos * 16, 16), pl.ds(0, width)],
                fps.at[k], fpr.at[k], device,
            ).start()
            return carry

        lax.fori_loop(0, PLANE - 1, one, 0)
        first_plane[k, :, pl.ds(pos * 16, 16), 0:width] = first_send[
            k, :, pl.ds(pos * 16, 16), 0:width
        ]

    def first_arrived(k):
        s, col, width, blocks = FORWARD[k]
        wait_bytes(first_plane.at[k, :, pl.ds(0, 240), pl.ds(0, width)], fpr.at[k])
        for h in range(2):
            rows = dot_nn(from_plane, first_plane[k, h, :, 0:width]).astype(BF16)
            ring_in[s, 2 * h : 2 * h + 2, 0:128, col : col + width] = rows.reshape(2, 128, width)
        across(k).start()

    def plane_send(k):
        s, col, width, blocks = FORWARD[k]
        send[s, :, col : col + width] = dot_nn(spread, stacked(k)).astype(BF16)

        def one(q, carry):
            there, device = plane_peer(q)
            remote(
                send.at[s, pl.ds(there * 16, 16), pl.ds(col, width)],
                plane_in.at[s, pl.ds(pos * 16, 16), pl.ds(col, width)],
                fps.at[k], fpr.at[k], device,
            ).start()
            return carry

        lax.fori_loop(0, PLANE - 1, one, 0)
        plane_in[s, pl.ds(pos * 16, 16), pl.ds(col, width)] = send[
            s, pl.ds(pos * 16, 16), pl.ds(col, width)
        ]

    for c in range(0, D - WIDE, WIDE):
        slot_rows(0, dispatch_t, acts_s, c)
    first_ring(0)
    first_ring(1)
    slot_rows(0, dispatch_t, acts_s, D - WIDE)
    e = jnp.exp(logits - jnp.max(logits, axis=1, keepdims=True))
    combine = e / jnp.sum(e, axis=1, keepdims=True)
    comb[...] = combine
    combine_t = split(combine.T)
    load_og.wait()
    for c in range(0, D, WIDE):
        og_s[0, :, c : c + WIDE], og_s[1, :, c : c + WIDE] = split(og[:, c : c + WIDE])
        slot_rows(1, combine_t, og_s, c)
        if c == 512:
            plane_send(2)
    for k in range(3, NF):
        plane_send(k)

    def ring_send(k):
        s, col, width, blocks = FORWARD[k]
        wait_bytes(plane_in.at[s, pl.ds(0, 240), pl.ds(col, width)], fpr.at[k])
        moved = dot_nn(regroup, plane_in[s, :, col : col + width])
        ring_out[s, :, :, col : col + width] = moved.astype(BF16).reshape(16, 16, width)

        def one(q, carry):
            there, lo, device = ring_peer(q)
            remote(
                ring_out.at[s, pl.ds(lo * 4, 4), :, pl.ds(col, width)],
                ring_in.at[s, :, pl.ds(z * 16, 16), pl.ds(col, width)],
                fzs.at[k], fzr.at[k], device,
            ).start()
            return carry

        lax.fori_loop(0, RING - 1, one, 0)
        ring_in[s, :, pl.ds(z * 16, 16), pl.ds(col, width)] = ring_out[
            s, pl.ds(z_lo * 4, 4), :, pl.ds(col, width)
        ]

    ring_send(2)
    first_spread(0)
    for k in range(3, NF):
        ring_send(k)

    load_so.wait()
    for k, part_of in enumerate(split(so[...])):
        so_s[k] = dot_nn(to_order_t, part_of).astype(BF16)
    comb_grad = three(dot_nt, (og_s[0], og_s[1]), (so_s[0], so_s[1]))
    combine = comb[...]
    comb_term[...] = combine * (
        comb_grad - jnp.sum(comb_grad * combine, axis=1, keepdims=True)
    )

    load_wi.wait()
    load_wo.wait()

    def ring_arrived(k):
        s, col, width, blocks = FORWARD[k]
        wait_bytes(ring_in.at[s, :, pl.ds(0, 112), pl.ds(col, width)], fzr.at[k])
        across(k).start()

    def expert(k, begin=0, end=5):
        s, col, width, blocks = FORWARD[k]
        if begin == 0:
            across(k).wait_recv()

        def tile(t):
            c = t * 256
            sums = [None, None]
            for kind in range(2):
                which = [j for j in range(4) if blocks[j][0] == kind]
                if not which:
                    continue
                rows = [ring_in[s, j, :, col : col + width] for j in which]
                rows = rows[0] if len(rows) == 1 else jnp.concatenate(rows, axis=1)
                span = pl.ds(blocks[which[0]][1], width * len(which))
                if kind == 0:
                    sums[0] = dot_nn(rows, wi[span, pl.ds(c, 256)])
                else:
                    sums[1] = dot_nt(rows, wo[pl.ds(c, 256), span])
            here = pl.ds(c, 256)
            if blocks is BLOCKS_A or blocks is BLOCKS_A1:
                acc[0, s, :, here] = sums[0]
            elif blocks is BLOCKS_A2:
                acc[0, s, :, here] += sums[0]
            elif blocks is BLOCKS_B:
                acc[0, s, :, here] = gelu_slope(acc[0, s, :, here] + sums[0])
                acc[1, s, :, here] = sums[1]
            else:
                hidden_grad = acc[1, s, :, here] + sums[1]
                pre_grad[s, :, here] = (hidden_grad * acc[0, s, :, here]).astype(BF16)

        for t in range(begin, end):
            tile(t)

    def back_across(s, b):
        col, width = BACK[b]
        return remote(
            part.at[s, :, pl.ds(128, 128), pl.ds(col, width)],
            part_in.at[s, :, :, pl.ds(col, width)],
            bcs.at[s, b], bcr.at[s, b], other,
        )

    def expert_back(s, b):
        col, width = BACK[b]
        weights = [wi[h * HALF + col : h * HALF + col + width, :] for h in range(2)]
        if width == 128:
            rows = dot_nt(pre_grad[s], jnp.concatenate(weights, axis=0))
            for h in range(2):
                part[s, h, :, col : col + width] = rows[:, h * width : h * width + width]
        else:
            for h in range(2):
                part[s, h, :, col : col + width] = dot_nt(pre_grad[s], weights[h])
        back_across(s, b).start()

    def back_ring(s, b):
        col, width = BACK[b]
        back_across(s, b).wait_recv()
        both = part[s, :, 0:128, col : col + width] + part_in[s, :, :, col : col + width]
        back_out[s, :, :, col : col + width] = both.astype(BF16)

        def one(q, carry):
            there, _, device = ring_peer(q)
            remote(
                back_out.at[s, :, pl.ds(there * 16, 16), pl.ds(col, width)],
                back_in.at[s, :, pl.ds(z * 16, 16), pl.ds(col, width)],
                bzs.at[s, b], bzr.at[s, b], device,
            ).start()
            return carry

        lax.fori_loop(0, RING - 1, one, 0)
        back_in[s, :, pl.ds(z * 16, 16), pl.ds(col, width)] = back_out[
            s, :, pl.ds(z * 16, 16), pl.ds(col, width)
        ]

    def back_plane(s, b):
        col, width = BACK[b]
        wait_bytes(back_in.at[s, :, pl.ds(0, 112), pl.ds(col, width)], bzr.at[s, b])
        back_send[s, :, col : col + width] = dot_nn(
            collect, back_in[s, :, :, col : col + width].reshape(ROWS, width)
        )

        def one(q, carry):
            there, device = plane_peer(q)
            remote(
                back_send.at[s, pl.ds(there * 8, 8), pl.ds(col, width)],
                sig.at[s, pl.ds(pos * 8, 8), pl.ds(col, width)],
                bps.at[s, b], bpr.at[s, b], device,
            ).start()
            return carry

        lax.fori_loop(0, PLANE - 1, one, 0)
        sig[s, pl.ds(pos * 8, 8), pl.ds(col, width)] = back_send[
            s, pl.ds(pos * 8, 8), pl.ds(col, width)
        ]

    def arrived(s, b):
        col, width = BACK[b]
        wait_bytes(sig.at[s, pl.ds(0, 120), pl.ds(col, width)], bpr.at[s, b])
        high, low = split(sig[s, :, col : col + width])
        for h in range(2):
            c = h * HALF + col
            there = place(s, h)
            grad = (dot_nn(there, high).astype(BF16), dot_nn(there, low).astype(BF16))
            tokens = (acts_s[0, :, c : c + width], acts_s[1, :, c : c + width])
            term = three(dot_nt, tokens, grad)
            if s == 0 and b == 0 and h == 0:
                disp_grad[...] = term
            else:
                disp_grad[...] += term
            for k in range(2):
                grad_s[k, s * 64 : s * 64 + 64, c : c + width] = grad[k][s * 64 : s * 64 + 64]

    def proj_across(s):
        return remote(dp_out.at[s], dp_in.at[s], dps.at[s, 0], dpr.at[s, 0], other)

    def proj_start(s):
        dispatch = disp[...]
        grad = disp_grad[...]
        whole = comb_term[...] + dispatch * (
            grad - jnp.sum(grad * dispatch, axis=0, keepdims=True)
        )
        logit_grad[...] = whole
        rows = [dot_nn(twice(s), a).astype(BF16) for a in split(whole.T)]
        upper = lax.rem(lax.div(iota2((SLOTS, 384), 0), 4), 2) == 0

        def half(which):
            terms = []
            for k in range(2):
                cols = pl.ds(pl.multiple_of(k * HALF + which * 256, 128), 384)
                terms.append(three(dot_nn, rows, (acts_s[0, :, cols], acts_s[1, :, cols])))
            return jnp.where(upper, terms[0], terms[1])

        dp_out[s] = half(1 - core)
        proj_across(s).start()
        dp_own[s] = half(core)

    def proj_plane(s):
        proj_across(s).wait_recv()
        dp_sum[s] = dp_own[s] + dp_in[s]

        def one(q, carry):
            there, device = plane_peer(q)
            remote(
                dp_sum.at[s, pl.ds(there * 8, 8)], dp_plane.at[s, pl.ds(pos * 8, 8)],
                dps.at[s, 1], dpr.at[s, 1], device,
            ).start()
            return carry

        lax.fori_loop(0, PLANE - 1, one, 0)
        dp_plane[s, pl.ds(pos * 8, 8)] = dp_sum[s, pl.ds(pos * 8, 8)]

    def proj_pack(s):
        wait_bytes(dp_plane.at[s, pl.ds(0, 120)], dpr.at[s, 1])
        total = jnp.sum(dp_plane[s].reshape(PLANE, 8, 384), axis=0)
        for k in range(3):
            dp_pack[:, s * 3 + k, :] = total[:, k * 128 : k * 128 + 128]

    def proj_ring():
        def one(q, carry):
            there, _, device = ring_peer(q)
            remote(
                dp_pack.at[there], dp_back.at[z], dps.at[0, 2], dpr.at[0, 2], device
            ).start()
            return carry

        lax.fori_loop(0, RING - 1, one, 0)
        dp_back[z] = dp_pack[z]

    def proj_end():
        wait_bytes(dp_back.at[pl.ds(0, 7)], dpr.at[0, 2])
        total = jnp.sum(dp_back[...], axis=0)
        for s in range(2):
            mine = jnp.concatenate([total[s * 3 + k : s * 3 + k + 1] for k in range(3)], axis=1)
            dproj_ref[s : s + 1, :] = jnp.where(core == 0, mine[:, 0:320], mine[:, 64:384])

    first_spread(1)
    first_arrived(0)
    ring_arrived(2)
    expert(0)
    first_arrived(1)
    ring_arrived(3)
    expert(2)
    expert(1)
    expert(3)
    ring_arrived(4)
    for b in range(NB):
        expert_back(0, b)
    expert(4)
    ring_arrived(5)
    for b in range(NB):
        back_ring(0, b)
    expert(5, 0, 3)
    ring_arrived(6)
    expert(5, 3, 5)
    expert(6)
    for b in range(NB):
        expert_back(1, b)
        if b > 0:
            back_ring(1, b - 1)
    back_ring(1, NB - 1)
    for b in range(NB):
        back_plane(0, b)
    back_plane(1, 0)
    back_plane(1, 1)
    arrived(0, 0)
    arrived(0, 1)
    back_plane(1, 2)
    arrived(0, 2)
    back_plane(1, 3)
    arrived(0, 3)
    proj_start(0)
    arrived(1, 0)
    proj_plane(0)
    arrived(1, 1)
    arrived(1, 2)
    arrived(1, 3)
    proj_start(1)
    proj_plane(1)
    proj_pack(0)
    whole = split(logit_grad[...])
    for c in range(0, D, 256):
        dacts[:, c : c + 256] = three(
            dot_nn, (disp_s[0], disp_s[1]), (grad_s[0, :, c : c + 256], grad_s[1, :, c : c + 256])
        ) + three(dot_nt, whole, (sp_s[0, c : c + 256, :], sp_s[1, c : c + 256, :]))
    proj_pack(1)
    proj_ring()
    proj_end()

    for k in range(NF):
        s, col, width, blocks = FORWARD[k]
        if k < 2:
            wait_bytes(first_plane.at[k, :, pl.ds(0, 240), pl.ds(0, width)], fps.at[k])
            wait_bytes(first_in.at[k, :, pl.ds(0, 112), pl.ds(0, width)], fzs.at[k])
        else:
            wait_bytes(plane_in.at[s, pl.ds(0, 240), pl.ds(col, width)], fps.at[k])
            wait_bytes(ring_in.at[s, :, pl.ds(0, 112), pl.ds(col, width)], fzs.at[k])
        across(k).wait_send()
    for s in range(2):
        for b in range(NB):
            col, width = BACK[b]
            back_across(s, b).wait_send()
            wait_bytes(back_in.at[s, :, pl.ds(0, 112), pl.ds(col, width)], bzs.at[s, b])
            wait_bytes(sig.at[s, pl.ds(0, 120), pl.ds(col, width)], bps.at[s, b])
        proj_across(s).wait_send()
        wait_bytes(dp_plane.at[s, pl.ds(0, 120)], dps.at[s, 1])
    wait_bytes(dp_back.at[pl.ds(0, 7)], dps.at[0, 2])


def deliver(dacts, dproj, dacts_hbm, dproj_hbm, sem):
    copies = [
        pltpu.make_async_copy(dacts, dacts_hbm, sem.at[0]),
        pltpu.make_async_copy(dproj, dproj_hbm, sem.at[1]),
    ]
    for copy in copies:
        copy.start()
    for copy in copies:
        copy.wait()


def local(activations, out_grad, slot_out, slot_proj, w_in, w_out):
    vmem = pltpu.VMEM
    sems = pltpu.SemaphoreType.DMA
    any_space = pl.BlockSpec(memory_space=pl.ANY)
    d_acts, d_proj = pl.pallas_call(
        kernel,
        out_shape=(
            pltpu.VMEM((TOKENS, D), F32),
            pltpu.VMEM((2, 320), F32),
        ),
        in_specs=[any_space] * 6,
        out_specs=(pl.BlockSpec(memory_space=pltpu.VMEM),) * 2,
        scratch_shapes=[
            vmem((TOKENS, D), F32),
            vmem((TOKENS, D), F32),
            vmem((SLOTS, D), F32),
            vmem((D, SLOTS), F32),
            vmem((D, D), BF16),
            vmem((D, D), BF16),
            vmem((2, TOKENS, D), BF16),
            vmem((2, TOKENS, D), BF16),
            vmem((2, SLOTS, D), BF16),
            vmem((2, D, SLOTS), BF16),
            vmem((2, TOKENS, SLOTS), BF16),
            vmem((TOKENS, SLOTS), F32),
            vmem((TOKENS, SLOTS), F32),
            vmem((TOKENS, SLOTS), F32),
            vmem((TOKENS, SLOTS), F32),
            vmem((TOKENS, SLOTS), F32),
            vmem((2, SLOTS, D), BF16),
            vmem((2, SLOTS, D), BF16),
            vmem((2, ROWS, HALF), BF16),
            vmem((2, ROWS, HALF), BF16),
            vmem((2, 16, 16, HALF), BF16),
            vmem((2, 4, ROWS, HALF), BF16),
            vmem((2, 16, 16, WIDE), BF16),
            vmem((2, 4, 128, WIDE), BF16),
            vmem((2, 2, ROWS, WIDE), BF16),
            vmem((2, 2, ROWS, WIDE), BF16),
            vmem((2, 2, ROWS, D), F32),
            vmem((2, ROWS, D), BF16),
            vmem((2, 2, ROWS, HALF), F32),
            vmem((2, 2, 128, HALF), F32),
            vmem((2, 2, 128, HALF), BF16),
            vmem((2, 2, 128, HALF), BF16),
            vmem((2, SLOTS, HALF), F32),
            vmem((2, SLOTS, HALF), F32),
            vmem((2, SLOTS, 384), F32),
            vmem((2, SLOTS, 384), F32),
            vmem((2, SLOTS, 384), F32),
            vmem((2, SLOTS, 384), F32),
            vmem((2, SLOTS, 384), F32),
            vmem((8, 8, 128), F32),
            vmem((8, 8, 128), F32),
            sems((6,)),
            sems((NF,)), sems((NF,)), sems((NF,)), sems((NF,)), sems((NF,)), sems((NF,)),
            sems((2, NB)), sems((2, NB)), sems((2, NB)), sems((2, NB)), sems((2, NB)), sems((2, NB)),
            sems((2, 3)), sems((2, 3)),
        ],
        compiler_params=pltpu.CompilerParams(
            collective_id=0, has_side_effects=True, vmem_limit_bytes=56 * 2**20
        ),
        name="soft_moe_backward",
    )(activations[0], out_grad[0], slot_out[0], slot_proj, w_in[0], w_out[0])
    d_acts, d_proj = pl.pallas_call(
        deliver,
        out_shape=(
            jax.ShapeDtypeStruct((TOKENS, D), F32),
            jax.ShapeDtypeStruct((2, 320), F32),
        ),
        in_specs=[pl.BlockSpec(memory_space=pltpu.VMEM)] * 2,
        out_specs=(any_space,) * 2,
        scratch_shapes=[sems((2,))],
        compiler_params=pltpu.CompilerParams(vmem_limit_bytes=2**20),
        name="deliver",
    )(d_acts, d_proj)
    return d_acts[None], d_proj.T


def solution(mesh):
    placed = (
        P(("ep", "tp"), None, None),
        P(("ep", "tp"), None, None),
        P(("ep", "tp"), None, None),
        P(),
        P("ep", None, "tp"),
        P("ep", "tp", None),
    )
    return jax.shard_map(
        local,
        mesh=mesh,
        in_specs=placed,
        out_specs=(P(("ep", "tp"), None, None), P("tp", "ep")),
        check_vma=False,
    )
```

```python
import functools

import jax
import jax.numpy as jnp
from jax import lax
from jax.experimental import pallas as pl
from jax.experimental.pallas import tpu as pltpu
from jax.sharding import PartitionSpec as P

MESH = pl.DeviceIdType.MESH
F32 = jnp.float32
BF16 = jnp.bfloat16
D = 1280
HALF = 640
TOKENS = 256
SLOTS = 128
ROWS = 256
PLANE = 16
RING = 8
WIDE = 256
BLOCKS_A = ((0, 0), (0, 256), (0, 512), (0, 768))
BLOCKS_B = ((0, 1024), (1, 0), (1, 256), (1, 512))
BLOCKS_C = ((1, 768), (1, 896), (1, 1024), (1, 1152))
FORWARD = (
    (0, 0, 256, BLOCKS_A), (1, 0, 256, BLOCKS_A),
    (0, 256, 256, BLOCKS_B), (0, 512, 128, BLOCKS_C),
    (1, 256, 256, BLOCKS_B), (1, 512, 128, BLOCKS_C),
)
BACK = ((0, 128), (128, 256), (384, 128), (512, 128))
NF, NB = len(FORWARD), len(BACK)


def gelu_slope(pre_act):
    normal_cdf = 0.5 * (1.0 + lax.erf(pre_act * 0.7071067811865476))
    density = jnp.exp(-0.5 * pre_act * pre_act) * 0.3989422804014327
    return normal_cdf + pre_act * density


def dot_nn(a, b):
    return jnp.dot(a, b, preferred_element_type=F32)


def dot_nt(a, b):
    return lax.dot_general(a, b, (((1,), (1,)), ((), ())), preferred_element_type=F32)


def split(a):
    high = a.astype(BF16)
    return high, (a - high.astype(F32)).astype(BF16)


def three(dot, a, b):
    return dot(a[0], b[0]) + (dot(a[0], b[1]) + dot(a[1], b[0]))


def iota2(shape, axis):
    return lax.broadcasted_iota(jnp.int32, shape, axis)


def one_hot(condition):
    return jnp.where(condition, 1.0, 0.0).astype(BF16)


def kernel(
    acts_hbm, og_hbm, so_hbm, sp_hbm, wi_hbm, wo_hbm,
    dacts, dproj_ref,
    acts, og, so, sp, wi, wo,
    acts_s, og_s, so_s, sp_s, disp_s, disp, comb, comb_term, disp_grad, logit_grad, grad_s,
    slots, send, plane_in, ring_out, ring_in, first_out, first_in, first_send, first_plane,
    acc, pre_grad, part, part_in, back_out, back_in, back_send, sig,
    dp_out, dp_own, dp_in, dp_sum, dp_plane, dp_pack, dp_back,
    load_sem, fps, fpr, fzs, fzr, fcs, fcr, bcs, bcr, bzs, bzr, bps, bpr, dps, dpr,
):
    ep, tp = lax.axis_index("ep"), lax.axis_index("tp")
    z_lo, pos = lax.div(ep, 16), lax.rem(ep, 16)
    x, y = lax.div(pos, 4), lax.rem(pos, 4)
    z_hi, core = lax.div(tp, 2), lax.rem(tp, 2)
    z = z_hi * 4 + z_lo
    other = {"ep": ep, "tp": z_hi * 2 + (1 - core)}

    def plane_peer(i):
        q = 1 + lax.rem(i + 8, PLANE - 1)
        there = lax.rem(x + lax.div(q, 4), 4) * 4 + lax.rem(y + lax.rem(q, 4), 4)
        return there, {"ep": z_lo * 16 + there, "tp": tp}

    def ring_peer(i):
        q = 1 + lax.rem(i + 2, RING - 1)
        there = lax.rem(z + q, RING)
        lo = lax.rem(there, 4)
        return there, lo, {"ep": lo * 16 + pos, "tp": lax.div(there, 4) * 2 + core}

    def remote(src, dst, send_sem, recv_sem, device):
        return pltpu.make_async_remote_copy(
            src_ref=src, dst_ref=dst, send_sem=send_sem, recv_sem=recv_sem,
            device_id=device, device_id_type=MESH,
        )

    def wait_bytes(ref, sem):
        pltpu.make_async_copy(ref, ref, sem).wait()

    loads = []
    pairs = ((sp_hbm, sp), (acts_hbm, acts), (og_hbm, og), (so_hbm, so), (wi_hbm, wi), (wo_hbm, wo))
    for k, (src, dst) in enumerate(pairs):
        loads.append(pltpu.make_async_copy(src, dst, load_sem.at[k]))
        if k < 2:
            loads[-1].start()
    load_sp, load_acts, load_og, load_so, load_wi, load_wo = loads

    barrier = pltpu.get_barrier_semaphore()

    def greet_plane(q, carry):
        pl.semaphore_signal(barrier, inc=1, device_id=plane_peer(q)[1], device_id_type=MESH)
        return carry

    def greet_ring(q, carry):
        pl.semaphore_signal(barrier, inc=1, device_id=ring_peer(q)[2], device_id_type=MESH)
        return carry

    lax.fori_loop(0, RING - 1, greet_ring, 0)
    lax.fori_loop(0, PLANE - 1, greet_plane, 0)
    pl.semaphore_signal(barrier, inc=1, device_id=other, device_id_type=MESH)

    n, r = iota2((SLOTS, SLOTS), 0), iota2((SLOTS, SLOTS), 1)
    to_order = one_hot(n == lax.rem(r, 4) * 32 + lax.rem(lax.div(r, 4), 16) * 2 + lax.div(r, 64))
    to_order_t = one_hot(r == lax.rem(n, 4) * 32 + lax.rem(lax.div(n, 4), 16) * 2 + lax.div(n, 64))
    o, i = iota2((ROWS, ROWS), 0), iota2((ROWS, ROWS), 1)
    spread = one_hot(
        i == lax.rem(lax.div(o, 4), 4) * 64 + lax.div(o, 16) * 4 + lax.rem(o, 4)
    )
    regroup = one_hot(
        i == lax.rem(o, 16) * 16 + lax.rem(lax.div(o, 16), 4) * 4 + lax.div(o, 64)
    )
    direct = one_hot(
        i == lax.rem(lax.div(o, 16), 4) * 64 + lax.rem(o, 16) * 4 + lax.div(o, 64)
    )
    to_plane = one_hot(
        i == lax.rem(lax.div(o, 8), 2) * 128 + lax.rem(o, 8) * 16 + lax.div(o, 16)
    )
    from_plane = one_hot(
        o == lax.rem(lax.div(i, 8), 2) * 128 + lax.rem(i, 8) * 16 + lax.div(i, 16)
    )
    o, i = iota2((SLOTS, ROWS), 0), iota2((SLOTS, ROWS), 1)
    collect = one_hot(
        (lax.div(i, 128) == lax.rem(lax.div(o, 4), 2))
        & (lax.rem(i, 64) == lax.rem(o, 4) * 16 + lax.div(o, 8))
    )
    def place(s, h):
        return one_hot(
            (lax.div(n, 64) == s)
            & (r == lax.div(lax.rem(n, 64), 4) * 8 + h * 4 + lax.rem(n, 4))
        )

    def twice(s):
        return one_hot(r == s * 64 + lax.div(n, 8) * 4 + lax.rem(n, 4))

    load_sp.wait()
    load_og.start()
    for k, part_of in enumerate(split(sp[...])):
        sp_s[k] = dot_nn(part_of, to_order).astype(BF16)
    load_acts.wait()
    for late in (load_so, load_wi, load_wo):
        late.start()
    acts_s[0], acts_s[1] = split(acts[...])
    logits = three(dot_nn, (acts_s[0], acts_s[1]), (sp_s[0], sp_s[1]))
    e = jnp.exp(logits - jnp.max(logits, axis=0, keepdims=True))
    dispatch = e / jnp.sum(e, axis=0, keepdims=True)
    disp[...] = dispatch
    disp_s[0], disp_s[1] = split(dispatch)
    dispatch_t = split(dispatch.T)

    def slot_rows(kind, weights_t, values, c):
        rows = three(dot_nn, weights_t, (values[0, :, c : c + WIDE], values[1, :, c : c + WIDE]))
        slots[kind, :, c : c + WIDE] = rows.astype(BF16)

    def across(k):
        s, col, width, blocks = FORWARD[k]
        return remote(
            ring_in.at[s, :, pl.ds(0, 128), pl.ds(col, width)],
            ring_in.at[s, :, pl.ds(128, 128), pl.ds(col, width)],
            fcs.at[k], fcr.at[k], other,
        )

    def stacked(k):
        s, col, width, blocks = FORWARD[k]
        parts = [
            slots[kind, s * 64 : s * 64 + 64, c : c + width] for kind, c in blocks
        ]
        return jnp.concatenate(parts, axis=0)

    def first_ring(k):
        width = FORWARD[k][2]
        rows = dot_nn(direct, stacked(k)).astype(BF16)
        first_out[k, :, :, 0:width] = rows.reshape(16, 16, width)
        if k == 0:
            pl.semaphore_wait(barrier, PLANE - 1 + RING - 1 + 1)

        def one(q, carry):
            there, lo, device = ring_peer(q)
            remote(
                first_out.at[k, pl.ds(lo * 4, 4), :, pl.ds(0, width)],
                first_in.at[k, :, pl.ds(z * 16, 16), pl.ds(0, width)],
                fzs.at[k], fzr.at[k], device,
            ).start()
            return carry

        lax.fori_loop(0, RING - 1, one, 0)
        first_in[k, :, pl.ds(z * 16, 16), 0:width] = first_out[k, pl.ds(z_lo * 4, 4), :, 0:width]

    def first_spread(k):
        width = FORWARD[k][2]
        wait_bytes(first_in.at[k, :, pl.ds(0, 112), pl.ds(0, width)], fzr.at[k])
        for h in range(2):
            rows = first_in[k, 2 * h : 2 * h + 2, :, 0:width].reshape(ROWS, width)
            first_send[k, h, :, 0:width] = dot_nn(to_plane, rows).astype(BF16)

        def one(q, carry):
            there, device = plane_peer(q)
            remote(
                first_send.at[k, :, pl.ds(there * 16, 16), pl.ds(0, width)],
                first_plane.at[k, :, pl.ds(pos * 16, 16), pl.ds(0, width)],
                fps.at[k], fpr.at[k], device,
            ).start()
            return carry

        lax.fori_loop(0, PLANE - 1, one, 0)
        first_plane[k, :, pl.ds(pos * 16, 16), 0:width] = first_send[
            k, :, pl.ds(pos * 16, 16), 0:width
        ]

    def first_arrived(k):
        s, col, width, blocks = FORWARD[k]
        wait_bytes(first_plane.at[k, :, pl.ds(0, 240), pl.ds(0, width)], fpr.at[k])
        for h in range(2):
            rows = dot_nn(from_plane, first_plane[k, h, :, 0:width]).astype(BF16)
            ring_in[s, 2 * h : 2 * h + 2, 0:128, col : col + width] = rows.reshape(2, 128, width)
        across(k).start()

    def plane_send(k):
        s, col, width, blocks = FORWARD[k]
        send[s, :, col : col + width] = dot_nn(spread, stacked(k)).astype(BF16)

        def one(q, carry):
            there, device = plane_peer(q)
            remote(
                send.at[s, pl.ds(there * 16, 16), pl.ds(col, width)],
                plane_in.at[s, pl.ds(pos * 16, 16), pl.ds(col, width)],
                fps.at[k], fpr.at[k], device,
            ).start()
            return carry

        lax.fori_loop(0, PLANE - 1, one, 0)
        plane_in[s, pl.ds(pos * 16, 16), pl.ds(col, width)] = send[
            s, pl.ds(pos * 16, 16), pl.ds(col, width)
        ]

    for c in range(0, D - WIDE, WIDE):
        slot_rows(0, dispatch_t, acts_s, c)
    first_ring(0)
    first_ring(1)
    slot_rows(0, dispatch_t, acts_s, D - WIDE)
    e = jnp.exp(logits - jnp.max(logits, axis=1, keepdims=True))
    combine = e / jnp.sum(e, axis=1, keepdims=True)
    comb[...] = combine
    combine_t = split(combine.T)
    load_og.wait()
    for c in range(0, D, WIDE):
        og_s[0, :, c : c + WIDE], og_s[1, :, c : c + WIDE] = split(og[:, c : c + WIDE])
        slot_rows(1, combine_t, og_s, c)
        if c == 512:
            plane_send(2)
    for k in range(3, NF):
        plane_send(k)

    def ring_send(k):
        s, col, width, blocks = FORWARD[k]
        wait_bytes(plane_in.at[s, pl.ds(0, 240), pl.ds(col, width)], fpr.at[k])
        moved = dot_nn(regroup, plane_in[s, :, col : col + width])
        ring_out[s, :, :, col : col + width] = moved.astype(BF16).reshape(16, 16, width)

        def one(q, carry):
            there, lo, device = ring_peer(q)
            remote(
                ring_out.at[s, pl.ds(lo * 4, 4), :, pl.ds(col, width)],
                ring_in.at[s, :, pl.ds(z * 16, 16), pl.ds(col, width)],
                fzs.at[k], fzr.at[k], device,
            ).start()
            return carry

        lax.fori_loop(0, RING - 1, one, 0)
        ring_in[s, :, pl.ds(z * 16, 16), pl.ds(col, width)] = ring_out[
            s, pl.ds(z_lo * 4, 4), :, pl.ds(col, width)
        ]

    ring_send(2)
    first_spread(0)
    for k in range(3, NF):
        ring_send(k)

    dp_pack[...] = jnp.zeros_like(dp_pack)
    load_so.wait()
    for k, part_of in enumerate(split(so[...])):
        so_s[k] = dot_nn(to_order_t, part_of).astype(BF16)
    comb_grad = three(dot_nt, (og_s[0], og_s[1]), (so_s[0], so_s[1]))
    combine = comb[...]
    comb_term[...] = combine * (
        comb_grad - jnp.sum(comb_grad * combine, axis=1, keepdims=True)
    )

    load_wi.wait()
    load_wo.wait()

    def ring_arrived(k):
        s, col, width, blocks = FORWARD[k]
        wait_bytes(ring_in.at[s, :, pl.ds(0, 112), pl.ds(col, width)], fzr.at[k])
        across(k).start()

    def expert(k, begin=0, end=5):
        s, col, width, blocks = FORWARD[k]
        if begin == 0:
            across(k).wait_recv()

        def tile(t):
            c = t * 256
            sums = [None, None]
            for kind in range(2):
                which = [j for j in range(4) if blocks[j][0] == kind]
                if not which:
                    continue
                rows = [ring_in[s, j, :, col : col + width] for j in which]
                rows = rows[0] if len(rows) == 1 else jnp.concatenate(rows, axis=1)
                span = pl.ds(blocks[which[0]][1], width * len(which))
                if kind == 0:
                    sums[0] = dot_nn(rows, wi[span, pl.ds(c, 256)])
                else:
                    sums[1] = dot_nt(rows, wo[pl.ds(c, 256), span])
            here = pl.ds(c, 256)
            if blocks is BLOCKS_A:
                acc[0, s, :, here] = sums[0]
            elif blocks is BLOCKS_B:
                acc[0, s, :, here] = gelu_slope(acc[0, s, :, here] + sums[0])
                acc[1, s, :, here] = sums[1]
            else:
                hidden_grad = acc[1, s, :, here] + sums[1]
                pre_grad[s, :, here] = (hidden_grad * acc[0, s, :, here]).astype(BF16)

        for t in range(begin, end):
            tile(t)

    def back_across(s, b):
        col, width = BACK[b]
        return remote(
            part.at[s, :, pl.ds(128, 128), pl.ds(col, width)],
            part_in.at[s, :, :, pl.ds(col, width)],
            bcs.at[s, b], bcr.at[s, b], other,
        )

    def expert_back(s, b):
        col, width = BACK[b]
        weights = [wi[h * HALF + col : h * HALF + col + width, :] for h in range(2)]
        if width == 128:
            rows = dot_nt(pre_grad[s], jnp.concatenate(weights, axis=0))
            for h in range(2):
                part[s, h, :, col : col + width] = rows[:, h * width : h * width + width]
        else:
            for h in range(2):
                part[s, h, :, col : col + width] = dot_nt(pre_grad[s], weights[h])
        back_across(s, b).start()

    def back_ring(s, b):
        col, width = BACK[b]
        back_across(s, b).wait_recv()
        both = part[s, :, 0:128, col : col + width] + part_in[s, :, :, col : col + width]
        back_out[s, :, :, col : col + width] = both.astype(BF16)

        def one(q, carry):
            there, _, device = ring_peer(q)
            remote(
                back_out.at[s, :, pl.ds(there * 16, 16), pl.ds(col, width)],
                back_in.at[s, :, pl.ds(z * 16, 16), pl.ds(col, width)],
                bzs.at[s, b], bzr.at[s, b], device,
            ).start()
            return carry

        lax.fori_loop(0, RING - 1, one, 0)
        back_in[s, :, pl.ds(z * 16, 16), pl.ds(col, width)] = back_out[
            s, :, pl.ds(z * 16, 16), pl.ds(col, width)
        ]

    def back_plane(s, b):
        col, width = BACK[b]
        wait_bytes(back_in.at[s, :, pl.ds(0, 112), pl.ds(col, width)], bzr.at[s, b])
        back_send[s, :, col : col + width] = dot_nn(
            collect, back_in[s, :, :, col : col + width].reshape(ROWS, width)
        )

        def one(q, carry):
            there, device = plane_peer(q)
            remote(
                back_send.at[s, pl.ds(there * 8, 8), pl.ds(col, width)],
                sig.at[s, pl.ds(pos * 8, 8), pl.ds(col, width)],
                bps.at[s, b], bpr.at[s, b], device,
            ).start()
            return carry

        lax.fori_loop(0, PLANE - 1, one, 0)
        sig[s, pl.ds(pos * 8, 8), pl.ds(col, width)] = back_send[
            s, pl.ds(pos * 8, 8), pl.ds(col, width)
        ]

    def arrived(s, b):
        col, width = BACK[b]
        wait_bytes(sig.at[s, pl.ds(0, 120), pl.ds(col, width)], bpr.at[s, b])
        high, low = split(sig[s, :, col : col + width])
        for h in range(2):
            c = h * HALF + col
            there = place(s, h)
            grad = (dot_nn(there, high).astype(BF16), dot_nn(there, low).astype(BF16))
            tokens = (acts_s[0, :, c : c + width], acts_s[1, :, c : c + width])
            term = three(dot_nt, tokens, grad)
            if s == 0 and b == 0 and h == 0:
                disp_grad[...] = term
            else:
                disp_grad[...] += term
            for k in range(2):
                grad_s[k, s * 64 : s * 64 + 64, c : c + width] = grad[k][s * 64 : s * 64 + 64]

    def proj_across(s):
        return remote(dp_out.at[s], dp_in.at[s], dps.at[s, 0], dpr.at[s, 0], other)

    def proj_start(s):
        dispatch = disp[...]
        grad = disp_grad[...]
        whole = comb_term[...] + dispatch * (
            grad - jnp.sum(grad * dispatch, axis=0, keepdims=True)
        )
        logit_grad[...] = whole
        rows = [dot_nt(twice(s), a).astype(BF16) for a in split(whole)]
        upper = lax.rem(lax.div(iota2((SLOTS, 384), 0), 4), 2) == 0

        def half(which):
            terms = []
            for k in range(2):
                cols = pl.ds(pl.multiple_of(k * HALF + which * 256, 128), 384)
                terms.append(three(dot_nn, rows, (acts_s[0, :, cols], acts_s[1, :, cols])))
            return jnp.where(upper, terms[0], terms[1])

        dp_out[s] = half(1 - core)
        proj_across(s).start()
        dp_own[s] = half(core)

    def proj_plane(s):
        proj_across(s).wait_recv()
        dp_sum[s] = dp_own[s] + dp_in[s]

        def one(q, carry):
            there, device = plane_peer(q)
            remote(
                dp_sum.at[s, pl.ds(there * 8, 8)], dp_plane.at[s, pl.ds(pos * 8, 8)],
                dps.at[s, 1], dpr.at[s, 1], device,
            ).start()
            return carry

        lax.fori_loop(0, PLANE - 1, one, 0)
        dp_plane[s, pl.ds(pos * 8, 8)] = dp_sum[s, pl.ds(pos * 8, 8)]

    def proj_pack(s):
        wait_bytes(dp_plane.at[s, pl.ds(0, 120)], dpr.at[s, 1])
        total = jnp.sum(dp_plane[s].reshape(PLANE, 8, 384), axis=0)
        for k in range(3):
            dp_pack[:, s * 3 + k, :] = total[:, k * 128 : k * 128 + 128]

    def proj_ring():
        def one(q, carry):
            there, _, device = ring_peer(q)
            remote(
                dp_pack.at[there], dp_back.at[z], dps.at[0, 2], dpr.at[0, 2], device
            ).start()
            return carry

        lax.fori_loop(0, RING - 1, one, 0)
        dp_back[z] = dp_pack[z]

    def proj_end():
        wait_bytes(dp_back.at[pl.ds(0, 7)], dpr.at[0, 2])
        total = jnp.sum(dp_back[...], axis=0)
        for s in range(2):
            mine = jnp.concatenate([total[s * 3 + k : s * 3 + k + 1] for k in range(3)], axis=1)
            dproj_ref[s : s + 1, :] = jnp.where(core == 0, mine[:, 0:320], mine[:, 64:384])

    first_spread(1)
    first_arrived(0)
    expert(0)
    ring_arrived(2)
    first_arrived(1)
    expert(2)
    ring_arrived(3)
    expert(1)
    expert(3)
    for b in range(NB):
        expert_back(0, b)
    ring_arrived(4)
    for b in range(NB):
        back_ring(0, b)
    expert(4, 0, 3)
    ring_arrived(5)
    expert(4, 3, 5)
    expert(5)
    for b in range(NB):
        expert_back(1, b)
        if b > 0:
            back_ring(1, b - 1)
    back_ring(1, NB - 1)
    for b in range(NB):
        back_plane(0, b)
    back_plane(1, 0)
    back_plane(1, 1)
    arrived(0, 0)
    arrived(0, 1)
    back_plane(1, 2)
    arrived(0, 2)
    back_plane(1, 3)
    arrived(0, 3)
    proj_start(0)
    arrived(1, 0)
    proj_plane(0)
    arrived(1, 1)
    arrived(1, 2)
    arrived(1, 3)
    proj_start(1)
    proj_plane(1)
    proj_pack(0)
    whole = split(logit_grad[...])
    for c in range(0, D, 256):
        dacts[:, c : c + 256] = three(
            dot_nn, (disp_s[0], disp_s[1]), (grad_s[0, :, c : c + 256], grad_s[1, :, c : c + 256])
        ) + three(dot_nt, whole, (sp_s[0, c : c + 256, :], sp_s[1, c : c + 256, :]))
    proj_pack(1)
    proj_ring()
    proj_end()

    for k in range(NF):
        s, col, width, blocks = FORWARD[k]
        if k < 2:
            wait_bytes(first_plane.at[k, :, pl.ds(0, 240), pl.ds(0, width)], fps.at[k])
            wait_bytes(first_in.at[k, :, pl.ds(0, 112), pl.ds(0, width)], fzs.at[k])
        else:
            wait_bytes(plane_in.at[s, pl.ds(0, 240), pl.ds(col, width)], fps.at[k])
            wait_bytes(ring_in.at[s, :, pl.ds(0, 112), pl.ds(col, width)], fzs.at[k])
        across(k).wait_send()
    for s in range(2):
        for b in range(NB):
            col, width = BACK[b]
            back_across(s, b).wait_send()
            wait_bytes(back_in.at[s, :, pl.ds(0, 112), pl.ds(col, width)], bzs.at[s, b])
            wait_bytes(sig.at[s, pl.ds(0, 120), pl.ds(col, width)], bps.at[s, b])
        proj_across(s).wait_send()
        wait_bytes(dp_plane.at[s, pl.ds(0, 120)], dps.at[s, 1])
    wait_bytes(dp_back.at[pl.ds(0, 7)], dps.at[0, 2])


def deliver(dacts, dproj, dacts_hbm, dproj_hbm, sem):
    copies = [
        pltpu.make_async_copy(dacts, dacts_hbm, sem.at[0]),
        pltpu.make_async_copy(dproj, dproj_hbm, sem.at[1]),
    ]
    for copy in copies:
        copy.start()
    for copy in copies:
        copy.wait()


def local(activations, out_grad, slot_out, slot_proj, w_in, w_out):
    vmem = pltpu.VMEM
    sems = pltpu.SemaphoreType.DMA
    any_space = pl.BlockSpec(memory_space=pl.ANY)
    d_acts, d_proj = pl.pallas_call(
        kernel,
        out_shape=(
            pltpu.VMEM((TOKENS, D), F32),
            pltpu.VMEM((2, 320), F32),
        ),
        in_specs=[any_space] * 6,
        out_specs=(pl.BlockSpec(memory_space=pltpu.VMEM),) * 2,
        scratch_shapes=[
            vmem((TOKENS, D), F32),
            vmem((TOKENS, D), F32),
            vmem((SLOTS, D), F32),
            vmem((D, SLOTS), F32),
            vmem((D, D), BF16),
            vmem((D, D), BF16),
            vmem((2, TOKENS, D), BF16),
            vmem((2, TOKENS, D), BF16),
            vmem((2, SLOTS, D), BF16),
            vmem((2, D, SLOTS), BF16),
            vmem((2, TOKENS, SLOTS), BF16),
            vmem((TOKENS, SLOTS), F32),
            vmem((TOKENS, SLOTS), F32),
            vmem((TOKENS, SLOTS), F32),
            vmem((TOKENS, SLOTS), F32),
            vmem((TOKENS, SLOTS), F32),
            vmem((2, SLOTS, D), BF16),
            vmem((2, SLOTS, D), BF16),
            vmem((2, ROWS, HALF), BF16),
            vmem((2, ROWS, HALF), BF16),
            vmem((2, 16, 16, HALF), BF16),
            vmem((2, 4, ROWS, HALF), BF16),
            vmem((2, 16, 16, WIDE), BF16),
            vmem((2, 4, 128, WIDE), BF16),
            vmem((2, 2, ROWS, WIDE), BF16),
            vmem((2, 2, ROWS, WIDE), BF16),
            vmem((2, 2, ROWS, D), F32),
            vmem((2, ROWS, D), BF16),
            vmem((2, 2, ROWS, HALF), F32),
            vmem((2, 2, 128, HALF), F32),
            vmem((2, 2, 128, HALF), BF16),
            vmem((2, 2, 128, HALF), BF16),
            vmem((2, SLOTS, HALF), F32),
            vmem((2, SLOTS, HALF), F32),
            vmem((2, SLOTS, 384), F32),
            vmem((2, SLOTS, 384), F32),
            vmem((2, SLOTS, 384), F32),
            vmem((2, SLOTS, 384), F32),
            vmem((2, SLOTS, 384), F32),
            vmem((8, 8, 128), F32),
            vmem((8, 8, 128), F32),
            sems((6,)),
            sems((NF,)), sems((NF,)), sems((NF,)), sems((NF,)), sems((NF,)), sems((NF,)),
            sems((2, NB)), sems((2, NB)), sems((2, NB)), sems((2, NB)), sems((2, NB)), sems((2, NB)),
            sems((2, 3)), sems((2, 3)),
        ],
        compiler_params=pltpu.CompilerParams(
            collective_id=0, has_side_effects=True, vmem_limit_bytes=56 * 2**20
        ),
        name="soft_moe_backward",
    )(activations[0], out_grad[0], slot_out[0], slot_proj, w_in[0], w_out[0])
    d_acts, d_proj = pl.pallas_call(
        deliver,
        out_shape=(
            jax.ShapeDtypeStruct((TOKENS, D), F32),
            jax.ShapeDtypeStruct((2, 320), F32),
        ),
        in_specs=[pl.BlockSpec(memory_space=pltpu.VMEM)] * 2,
        out_specs=(any_space,) * 2,
        scratch_shapes=[sems((2,))],
        compiler_params=pltpu.CompilerParams(vmem_limit_bytes=2**20),
        name="deliver",
    )(d_acts, d_proj)
    return d_acts[None], d_proj.T


def solution(mesh):
    placed = (
        P(("ep", "tp"), None, None),
        P(("ep", "tp"), None, None),
        P(("ep", "tp"), None, None),
        P(),
        P("ep", None, "tp"),
        P("ep", "tp", None),
    )
    return jax.shard_map(
        local,
        mesh=mesh,
        in_specs=placed,
        out_specs=(P(("ep", "tp"), None, None), P("tp", "ep")),
        check_vma=False,
    )
```
